512 devices in a mesh: ctx: 32 (over x, z_hi, core), tp: 16 (over z_lo, y).
Axes of the slice: x: 4, y: 4, z: 16 (z_hi: 4, z_lo: 4; z = z_hi * 4 + z_lo), core: 2. Of those that a mesh axis runs over, the one named last changes fastest.
Arguments:
- residual_in: bfloat16 [8192, 6144], P(('ctx', 'tp')), may hold values from -1.5 to 1.5
- query_rows: bfloat16 [8192, 4096], P('ctx', 'tp'), may hold values from -60 to 60
- key_rows: bfloat16 [8192, 4096], P('ctx', 'tp'), may hold values from -6 to 6
- value_rows: bfloat16 [8192, 4096], P('ctx', 'tp'), may hold values from -48 to 48
- out_weight: bfloat16 [4096, 6144], P('tp'), may hold values from -0.09375 to 0.09375
- gate_table: bfloat16 [64, 6144], replicated, may hold values from 0.25 to 2
- stretch_order: int32 [4], replicated, may hold values from 0 to 3, each once
- noise_levels: int32 [4], replicated, may hold values from 0 to 63
Outputs:
- mixed: bfloat16 [8192, 6144], P(('ctx', 'tp'))
The draws below stay inside these ranges and needn't reach their ends.
Inputs may be any that keep to these rules, and one draw needn't show every extreme that they name: `stretch_order`: each place 0 to 3 once.
All inputs are finite; a program needn't handle non-finite values.
Results may differ from the reference program's by a relative error of at most 0.035.
Values may be sent and summed in bfloat16 or wider, within the bound.
A program may use at most 64 MiB of HBM per device.

```python
import math
import jax
import jax.numpy as jnp
from jax import lax

D = 6144
HEADS = 32
DH = 128
QROWS = 256
STRETCHES = 4
LEVELS = 64
TOKENS = 8192
HD = 4096
N_CTX = 32
N_TP = 16


def shared_keys(key):
    normal_part = jax.random.truncated_normal(jax.random.fold_in(key, 101), -6.0, 6.0, (TOKENS, HEADS * DH), jnp.float32)
    return normal_part


def draw_key_rows(key, part):
    return shared_keys(key).astype(jnp.bfloat16)


def draw_query_rows(key, part):
    key = jax.random.fold_in(key, 7)
    normal_rows = jax.random.truncated_normal(key, -6.0, 6.0, (TOKENS, HEADS * DH), jnp.float32)
    return (1.5 * normal_rows).astype(jnp.bfloat16)


def with_ends(result, own_key, least, top_value):
    extent = result.shape
    index_at = [jax.random.randint(jax.random.fold_in(own_key, axis), (), 0, extent[axis]) for axis in range(len(extent))]
    result = result.at[tuple(index_at)].set(least)
    longest = extent.index(max(extent))
    index_at[longest] = (index_at[longest] + 1) % extent[longest]
    return result.at[tuple(index_at)].set(top_value)


def block_scale(own_key, extent, pieces, least, largest):
    gain = 1.0
    for dim, shards_of in pieces:
        heights = jax.random.uniform(jax.random.fold_in(jax.random.fold_in(own_key, 6), dim), (shards_of,), jnp.float32, least / len(pieces), largest / len(pieces))
        gain = gain * jnp.repeat(jnp.exp(heights), extent[dim] // shards_of).reshape((-1,) + (1,) * (len(extent) - 1 - dim))
    return gain


def centred(key, dims, width, reach, split=(), kind=jnp.bfloat16):
    gain = block_scale(key, dims, split, -0.22, 0.18) if split else 1.0
    array = jax.random.normal(key, dims, jnp.float32) * width * gain
    return jnp.minimum(jnp.maximum(array, -reach), reach).astype(kind)


def setup_inputs(seed: int = 0) -> dict:
    key_list = jax.random.split(jax.random.key(seed), 9)
    return {
        "residual_in": centred(key_list[0], (TOKENS, D), 0.25, 1.5, ((0, 512),)),
        "query_rows": draw_query_rows(jax.random.fold_in(key_list[8], 71), 0),
        "key_rows": draw_key_rows(jax.random.fold_in(key_list[8], 71), 0),
        "value_rows": centred(key_list[3], (TOKENS, HD), 8.0, 48.0, ((0, 32), (1, 16))),
        "out_weight": centred(key_list[4], (HD, D), HD ** -0.5, 0.09375, ((0, 16),)),
        "gate_table": jnp.clip(jax.random.uniform(key_list[5], (LEVELS, D), jnp.float32, 0.25, 2.0), 0.25, 2.0).astype(jnp.bfloat16),
        "stretch_order": jax.random.permutation(key_list[6], STRETCHES).astype(jnp.int32),
        "noise_levels": with_ends(jax.random.randint(key_list[7], (STRETCHES,), 0, LEVELS), jax.random.fold_in(key_list[7], 1), 0, LEVELS - 1).astype(jnp.int32),
    }


NEG = -1e+30

def reference(residual_in, query_rows, key_rows, value_rows, out_weight, gate_table, stretch_order, noise_levels):
    span = QROWS * (N_CTX // STRETCHES)
    scale = 1.0 / math.sqrt(DH)
    positions = jnp.arange(TOKENS, dtype=jnp.int32)
    place = stretch_order[positions // span]
    blocksize = math.gcd(TOKENS, 512)

    def one_head(head):
        column = (head * DH).astype(jnp.int32)
        query_head = lax.dynamic_slice_in_dim(query_rows, column, DH, 1)
        key_head = lax.dynamic_slice_in_dim(key_rows, column, DH, 1)
        value_head = lax.dynamic_slice_in_dim(value_rows, column, DH, 1)

        def one_block(number):
            offset = (number * blocksize).astype(jnp.int32)
            query_block = lax.dynamic_slice_in_dim(query_head, offset, blocksize, 0)
            query_place = lax.dynamic_slice_in_dim(place, offset, blocksize, 0)
            scores = jnp.dot(query_block, key_head.T, preferred_element_type=jnp.float32) * scale
            visible = place[None, :] <= query_place[:, None]
            scores = jnp.where(visible, scores, NEG)
            peak = lax.optimization_barrier(jnp.max(scores, axis=1, keepdims=True))
            weights = jnp.where(visible, jnp.exp(scores - peak), 0.0)
            total = lax.optimization_barrier(jnp.sum(weights, axis=1, keepdims=True))
            summed = jnp.dot(weights.astype(jnp.bfloat16), value_head, preferred_element_type=jnp.float32)
            return (summed / total).astype(jnp.bfloat16)
        blocks_out = lax.map(one_block, jnp.arange(TOKENS // blocksize, dtype=jnp.int32))
        return blocks_out.reshape(TOKENS, DH)
    per_head = lax.map(one_head, jnp.arange(HEADS, dtype=jnp.int32))
    attended = jnp.transpose(per_head, (1, 0, 2)).reshape(TOKENS, HEADS * DH)
    shard_cols = HEADS * DH // N_TP

    def add_shard(carry, shard):
        offset = (shard * shard_cols).astype(jnp.int32)
        columns = lax.dynamic_slice_in_dim(attended, offset, shard_cols, 1)
        weight_rows = lax.dynamic_slice_in_dim(out_weight, offset, shard_cols, 0)
        partial_term = jnp.dot(columns, weight_rows, preferred_element_type=jnp.float32)
        partial_term = lax.optimization_barrier(partial_term.astype(jnp.bfloat16)).astype(jnp.float32)
        return (carry + partial_term, None)
    projected, ignored = lax.scan(add_shard, jnp.zeros((TOKENS, D), jnp.float32), jnp.arange(N_TP, dtype=jnp.int32))
    gate = gate_table[noise_levels[place]].astype(jnp.float32)
    return (residual_in.astype(jnp.float32) + gate * projected).astype(jnp.bfloat16)
```

```python
import math

import jax
import jax.numpy as jnp
from jax import lax
from jax.experimental import pallas as pl
from jax.experimental.pallas import tpu as pltpu
from jax.sharding import PartitionSpec as P

MESH = pl.DeviceIdType.MESH
DH = 128
NEG = -1e30
SCALE = math.log2(math.e) / math.sqrt(DH)
F32 = jnp.float32
BF16 = jnp.bfloat16


def remote(src, dst, sems, device):
    return pltpu.make_async_remote_copy(
        src_ref=src,
        dst_ref=dst,
        send_sem=sems[0],
        recv_sem=sems[1],
        device_id=device,
        device_id_type=MESH,
    )


def kernel(
    res_in,
    q_in,
    k_in,
    v_in,
    w_in,
    gate_in,
    order_ref,
    noise_ref,
    out_ref,
    qbuf,
    kbuf,
    vbuf,
    acc,
    lsum,
    peak,
    osend,
    lsend,
    oret,
    lret,
    abuf,
    wbuf,
    pbuf,
    rbuf,
    gbuf,
    gsel,
    resbuf,
    local_sem,
    sib_sem,
    par_sem,
    crs_sem,
    qx_sem,
    ox_sem,
    lx_sem,
    z_sem,
    a_sem,
    w_sem,
    wf_sem,
    r_sem,
):
    ctx = lax.axis_index("ctx")
    tp = lax.axis_index("tp")
    x = ctx // 8
    zh = (ctx // 2) % 4
    core = ctx % 2
    zl = tp // 4
    y = tp % 4
    head = zh // 2
    mine = pl.ds(pl.multiple_of(head * DH, DH), DH)
    other = pl.ds(pl.multiple_of((1 - head) * DH, DH), DH)
    sib = (ctx + 1 - 2 * core, tp)
    par = (ctx + 2 - 4 * (zh % 2), tp)
    crs = (ctx + 6 - 4 * zh, tp)
    rows = q_in.shape[0]
    half = rows // 2
    slab = wbuf.shape[1]

    def xpeer(dx):
        return (((x + dx) % 4) * 8 + zh * 2 + core, tp)

    def ypeer(dy):
        return (ctx, zl * 4 + (y + dy) % 4)

    def tpeer(dz, dy):
        return (ctx, ((zl + dz) % 4) * 4 + (y + dy) % 4)

    def columns(index):
        return pl.ds(pl.multiple_of(index * slab, slab), slab)

    locals_ = [
        pltpu.make_async_copy(q_in.at[:, mine], qbuf.at[0], local_sem.at[0]),
        pltpu.make_async_copy(k_in.at[:, mine], kbuf.at[0, 0], local_sem.at[1]),
        pltpu.make_async_copy(v_in.at[:, mine], vbuf.at[0, 0], local_sem.at[2]),
        pltpu.make_async_copy(w_in.at[:, columns(y)], wbuf.at[pl.ds(0, rows)], local_sem.at[3]),
        pltpu.make_async_copy(gate_in, gbuf, local_sem.at[4]),
        pltpu.make_async_copy(res_in, resbuf, local_sem.at[5]),
    ]
    for copy in locals_:
        copy.start()

    barrier = pltpu.get_barrier_semaphore()
    partners = [sib, par, crs] + [xpeer(dx) for dx in (1, 2, 3)]
    for partner in partners:
        pl.semaphore_signal(barrier, inc=1, device_id=partner, device_id_type=MESH)

    def greet(step, carry):
        pl.semaphore_signal(
            barrier, inc=1, device_id=tpeer(step // 4, step % 4), device_id_type=MESH
        )
        return carry

    lax.fori_loop(1, 16, greet, 0)
    pl.semaphore_wait(barrier, len(partners) + 15)

    q_cross = remote(q_in.at[:, other], qbuf.at[4], (crs_sem.at[0, 0], crs_sem.at[1, 0]), crs)
    k_cross = remote(k_in.at[:, other], kbuf.at[2, 0], (crs_sem.at[0, 1], crs_sem.at[1, 1]), crs)
    v_cross = remote(v_in.at[:, other], vbuf.at[2, 0], (crs_sem.at[0, 2], crs_sem.at[1, 2]), crs)
    k_pair = remote(k_in.at[:, mine], kbuf.at[1, 0], (par_sem.at[0, 0], par_sem.at[1, 0]), par)
    v_pair = remote(v_in.at[:, mine], vbuf.at[1, 0], (par_sem.at[0, 1], par_sem.at[1, 1]), par)
    k_far = remote(kbuf.at[2, 0], kbuf.at[3, 0], (par_sem.at[0, 2], par_sem.at[1, 2]), par)
    v_far = remote(vbuf.at[2, 0], vbuf.at[3, 0], (par_sem.at[0, 3], par_sem.at[1, 3]), par)

    def share(buf, role, number):
        src = buf.at[role, 0]
        if role == 0:
            src = (k_in if number == 0 else v_in).at[:, mine]
        index = 2 * role + number
        return remote(src, buf.at[role, 1], (sib_sem.at[0, index], sib_sem.at[1, index]), sib)

    k_share = [share(kbuf, role, 0) for role in range(4)]
    v_share = [share(vbuf, role, 1) for role in range(4)]

    def q_across(part, dx):
        index = part * 3 + dx - 1
        src = q_in.at[:, mine] if part == 0 else qbuf.at[4]
        return remote(
            src, qbuf.at[4 * part + dx], (qx_sem.at[0, index], qx_sem.at[1, index]), xpeer(dx)
        )

    def w_send(dy):
        own_half = pl.ds(pl.multiple_of(half * core, half), half)
        there = pl.ds(pl.multiple_of(dy * rows + half * core, half), half)
        return remote(
            w_in.at[own_half, columns((y + dy) % 4)],
            wbuf.at[there],
            (w_sem.at[0, dy - 1], w_sem.at[1, dy - 1]),
            ypeer(dy),
        )

    def w_share(dy):
        there = pl.ds(pl.multiple_of(dy * rows + half * core, half), half)
        return remote(wbuf.at[there], wbuf.at[there], (wf_sem.at[0, dy - 1], wf_sem.at[1, dy - 1]), sib)

    q_cross.start()
    k_pair.start()
    k_cross.start()
    v_pair.start()
    v_cross.start()
    k_share[0].start()
    v_share[0].start()
    for dx in (1, 2, 3):
        q_across(0, dx).start()
    for dy in (1, 2, 3):
        w_send(dy).start()

    def block(b, role):
        k = kbuf[role].reshape(2 * rows, DH)
        v = vbuf[role].reshape(2 * rows, DH)
        count = 2 * rows // DH
        for top in range(0, rows, half):
            at = pl.ds(top, half)
            s = (
                lax.dot_general(
                    qbuf[b, at], k, (((1,), (1,)), ((), ())), preferred_element_type=F32
                )
                * SCALE
            )
            top_now = jnp.max(s, axis=1, keepdims=True)
            if role == 0:
                m = jnp.broadcast_to(top_now, (half, DH))
            else:
                m = jnp.maximum(peak[b, at], top_now)
                fade = jnp.exp2(peak[b, at] - m)
            p = jnp.exp2(s - jnp.concatenate([m] * count, axis=1))
            total = p[:, :DH]
            for part in range(1, count):
                total = total + p[:, part * DH : (part + 1) * DH]
            summed = jnp.dot(p.astype(BF16), v, preferred_element_type=F32)
            if role > 0:
                total = total + lsum[b, at] * fade
                summed = summed + acc[b, at] * fade
            if role < 3:
                peak[b, at] = m
                lsum[b, at] = total
                acc[b, at] = summed
            else:
                total = jnp.broadcast_to(jnp.sum(total, axis=1, keepdims=True), (half, DH))
                osend[b, at] = (summed / total).astype(BF16)
                lse = m + jnp.log2(total)
                lsend[b, pl.ds(top // half, 1)] = lse.T[:1]

    def blocks(first, count, role):
        def step(i, carry):
            block(first + i, role)
            return carry

        lax.fori_loop(0, count, step, 0)

    locals_[0].wait()
    locals_[1].wait()
    locals_[2].wait()
    k_share[0].wait_recv()
    v_share[0].wait_recv()
    for dx in (1, 2, 3):
        q_across(0, dx).wait_recv()
    blocks(0, 4, 0)

    q_cross.wait_recv()
    for dx in (1, 2, 3):
        q_across(1, dx).start()

    locals_[4].wait()
    place = order_ref[x]
    level = noise_ref[0] * 0
    for slot in range(4):
        level = level + jnp.where(place == slot, noise_ref[slot], 0)
    levels = gbuf.shape[0]
    picker = (lax.broadcasted_iota(jnp.int32, (16, levels), 1) == level).astype(BF16)
    for piece in range(4):
        at = pl.ds(piece * slab, slab)
        gsel[:, at] = jnp.dot(picker, gbuf[:, at], preferred_element_type=F32)

    k_pair.wait_recv()
    k_share[1].start()
    v_pair.wait_recv()
    v_share[1].start()
    k_cross.wait_recv()
    k_far.start()
    k_share[2].start()
    for dx in (1, 2, 3):
        q_across(1, dx).wait_recv()
    blocks(4, 4, 0)
    k_share[1].wait_recv()
    v_share[1].wait_recv()
    blocks(0, 4, 1)
    v_cross.wait_recv()
    v_far.start()
    v_share[2].start()
    blocks(4, 4, 1)
    k_share[2].wait_recv()
    v_share[2].wait_recv()
    blocks(0, 8, 2)
    for dy in (1, 2, 3):
        w_send(dy).wait_recv()
        w_share(dy).start()
    k_far.wait_recv()
    k_share[3].start()
    v_far.wait_recv()
    v_share[3].start()
    k_share[3].wait_recv()
    v_share[3].wait_recv()

    def o_back(part, dx):
        index = part * 3 + dx - 1
        b = 4 * part + dx
        return remote(
            osend.at[b], oret.at[index], (ox_sem.at[0, index], ox_sem.at[1, index]), xpeer(4 - dx)
        )

    def l_back(part, dx):
        index = part * 3 + dx - 1
        b = 4 * part + dx
        return remote(
            lsend.at[b], lret.at[index], (lx_sem.at[0, index], lx_sem.at[1, index]), xpeer(4 - dx)
        )

    for part in (1, 0):

        def last(i, carry):
            block(4 * part + 1 + i, 3)
            l_back(part, 1 + i).start()
            o_back(part, 1 + i).start()
            return carry

        lax.fori_loop(0, 3, last, 0)
        block(4 * part, 3)

    def merged(part, top):
        at = pl.ds(top, half)
        line = pl.ds(top // half, 1)
        states = [(lsend[4 * part, line], osend[4 * part, at])]
        for dx in (1, 2, 3):
            index = part * 3 + dx - 1
            seen = order_ref[(x + dx) % 4] <= place
            states.append((jnp.where(seen, lret[index, line], NEG), oret[index, at]))
        top_lse = states[0][0]
        for lse, _ in states[1:]:
            top_lse = jnp.maximum(top_lse, lse)
        total = jnp.zeros((half, DH), F32)
        result = jnp.zeros((half, DH), F32)
        for lse, value in states:
            share_of = jnp.broadcast_to(jnp.exp2(lse - top_lse), (DH, DH)).T
            total = total + share_of
            result = result + share_of * value.astype(F32)
        return (result / total).astype(BF16)

    back = remote(
        osend.at[4], abuf.at[:, mine], (z_sem.at[0], z_sem.at[1]), crs
    )
    for dx in (1, 2, 3):
        l_back(1, dx).wait_recv()
        o_back(1, dx).wait_recv()
    for top in range(0, rows, half):
        osend[4, pl.ds(top, half)] = merged(1, top)
    back.start()

    def a_send(which, dy):
        index = which * 3 + dy - 1
        lane = head if which == 0 else 1 - head
        there = pl.ds(pl.multiple_of(dy * 2 * DH + lane * DH, DH), DH)
        return remote(
            abuf.at[:, mine if which == 0 else other],
            abuf.at[:, there],
            (a_sem.at[0, index], a_sem.at[1, index]),
            ypeer(dy),
        )

    for dx in (1, 2, 3):
        l_back(0, dx).wait_recv()
        o_back(0, dx).wait_recv()
    for top in range(0, rows, half):
        abuf[pl.ds(top, half), mine] = merged(0, top)
    for dy in (1, 2, 3):
        a_send(0, dy).start()
    back.wait_recv()
    for dy in (1, 2, 3):
        a_send(1, dy).start()

    locals_[3].wait()
    for dy in (1, 2, 3):
        w_share(dy).wait_recv()
    for dy in (1, 2, 3):
        a_send(0, dy).wait_recv()
        a_send(1, dy).wait_recv()

    piece_width = 256

    def project(i, carry):
        at = pl.ds(pl.multiple_of(i * piece_width, piece_width), piece_width)
        pbuf[:, at] = jnp.dot(abuf[...], wbuf[:, at], preferred_element_type=F32).astype(BF16)
        return carry

    lax.fori_loop(0, slab // piece_width, project, 0)

    def r_send(step):
        there = tpeer(step // 4, step % 4)
        first = pl.ds(pl.multiple_of(there[1] * 16, 16), 16)
        return remote(
            pbuf.at[first], rbuf.at[step], (r_sem.at[0, step], r_sem.at[1, step]), there
        )

    def r_start(step, carry):
        r_send(step).start()
        return carry

    lax.fori_loop(1, 16, r_start, 0)

    own_rows = pl.ds(pl.multiple_of(tp * 16, 16), 16)
    rbuf[0] = pbuf[own_rows]

    def r_wait(step, carry):
        r_send(step).wait_recv()
        return carry

    lax.fori_loop(1, 16, r_wait, 0)
    locals_[5].wait()
    for dy in range(4):
        at = columns((y + 4 - dy) % 4)
        projected = rbuf[dy].astype(F32)
        for dz in (1, 2, 3):
            projected = projected + rbuf[4 * dz + dy].astype(F32)
        mixed = resbuf[:, at].astype(F32) + gsel[:, at] * projected
        out_ref[:, at] = mixed.astype(BF16)

    for copy in [q_cross, k_cross, v_cross, k_pair, v_pair, k_far, v_far, back]:
        copy.wait_send()
    for copy in k_share + v_share:
        copy.wait_send()
    for step in (1, 2, 3):
        w_send(step).wait_send()
        w_share(step).wait_send()
        for part in (0, 1):
            q_across(part, step).wait_send()
            o_back(part, step).wait_send()
            l_back(part, step).wait_send()
            a_send(part, step).wait_send()

    def r_left(step, carry):
        r_send(step).wait_send()
        return carry

    lax.fori_loop(1, 16, r_left, 0)


def on_device(
    residual_in,
    query_rows,
    key_rows,
    value_rows,
    out_weight,
    gate_table,
    stretch_order,
    noise_levels,
):
    rows = query_rows.shape[0]
    width = residual_in.shape[1]
    slab = width // 4
    any_spec = pl.BlockSpec(memory_space=pl.ANY)
    smem_spec = pl.BlockSpec(memory_space=pltpu.SMEM)
    dma = pltpu.SemaphoreType.DMA
    return pl.pallas_call(
        kernel,
        out_shape=jax.ShapeDtypeStruct(residual_in.shape, BF16),
        in_specs=[any_spec] * 6 + [smem_spec] * 2,
        out_specs=pl.BlockSpec(memory_space=pltpu.VMEM),
        scratch_shapes=[
            pltpu.VMEM((8, rows, DH), BF16),
            pltpu.VMEM((4, 2, rows, DH), BF16),
            pltpu.VMEM((4, 2, rows, DH), BF16),
            pltpu.VMEM((8, rows, DH), F32),
            pltpu.VMEM((8, rows, DH), F32),
            pltpu.VMEM((8, rows, DH), F32),
            pltpu.VMEM((8, rows, DH), BF16),
            pltpu.VMEM((8, 8, DH), F32),
            pltpu.VMEM((6, rows, DH), BF16),
            pltpu.VMEM((6, 8, DH), F32),
            pltpu.VMEM((rows, 8 * DH), BF16),
            pltpu.VMEM((4 * rows, slab), BF16),
            pltpu.VMEM((rows, slab), BF16),
            pltpu.VMEM((16, 16, slab), BF16),
            pltpu.VMEM(gate_table.shape, BF16),
            pltpu.VMEM((16, width), F32),
            pltpu.VMEM(residual_in.shape, BF16),
            dma((6,)),
            dma((2, 8)),
            dma((2, 4)),
            dma((2, 3)),
            dma((2, 6)),
            dma((2, 6)),
            dma((2, 6)),
            dma((2,)),
            dma((2, 6)),
            dma((2, 3)),
            dma((2, 3)),
            dma((2, 16)),
        ],
        compiler_params=pltpu.CompilerParams(
            collective_id=0, has_side_effects=True, vmem_limit_bytes=48 * 1024 * 1024
        ),
        name="sublayer",
    )(
        residual_in,
        query_rows,
        key_rows,
        value_rows,
        out_weight,
        gate_table,
        stretch_order,
        noise_levels,
    )


def solution(mesh):
    placed = (
        P(("ctx", "tp"), None),
        P("ctx", "tp"),
        P("ctx", "tp"),
        P("ctx", "tp"),
        P("tp", None),
        P(),
        P(),
        P(),
    )
    return jax.shard_map(
        on_device, mesh=mesh, in_specs=placed, out_specs=P(("ctx", "tp"), None), check_vma=False
    )
```

```python
import functools
import math

import jax
import jax.numpy as jnp
from jax import lax
from jax.experimental import pallas as pl
from jax.experimental.pallas import tpu as pltpu
from jax.sharding import PartitionSpec as P

MESH = pl.DeviceIdType.MESH
DH = 128
NEG = -1e30
SCALE = math.log2(math.e) / math.sqrt(DH)
F32 = jnp.float32
BF16 = jnp.bfloat16


def remote(src, dst, sems, device):
    return pltpu.make_async_remote_copy(
        src_ref=src,
        dst_ref=dst,
        send_sem=sems[0],
        recv_sem=sems[1],
        device_id=device,
        device_id_type=MESH,
    )


def kernel(
    res_in,
    q_in,
    k_in,
    v_in,
    w_in,
    gate_in,
    order_ref,
    noise_ref,
    out_ref,
    qbuf,
    kbuf,
    vbuf,
    acc,
    lsum,
    peak,
    osend,
    lsend,
    oret,
    lret,
    zsend,
    abuf,
    wbuf,
    pbuf,
    rbuf,
    gbuf,
    gsel,
    resbuf,
    local_sem,
    sib_sem,
    par_sem,
    crs_sem,
    qx_sem,
    ox_sem,
    lx_sem,
    z_sem,
    a_sem,
    w_sem,
    wf_sem,
    r_sem,
):
    ctx = lax.axis_index("ctx")
    tp = lax.axis_index("tp")
    x = ctx // 8
    zh = (ctx // 2) % 4
    core = ctx % 2
    zl = tp // 4
    y = tp % 4
    odd = zl % 2
    ring = (zh + odd) % 4
    head = ring // 2
    mine = pl.ds(pl.multiple_of(head * DH, DH), DH)
    other = pl.ds(pl.multiple_of((1 - head) * DH, DH), DH)

    def at_ring(place):
        return (x * 8 + ((place + 4 - odd) % 4) * 2 + core, tp)

    sib = (ctx + 1 - 2 * core, tp)
    par = at_ring(ring + 1 - 2 * (ring % 2))
    crs = at_ring(3 - ring)
    rows = k_in.shape[0]
    half = rows // 2
    slab = wbuf.shape[1]

    def xpeer(dx):
        return (((x + dx) % 4) * 8 + zh * 2 + core, tp)

    def ypeer(dy):
        return (ctx, zl * 4 + (y + dy) % 4)

    def tpeer(dz, dy):
        return (ctx, ((zl + dz) % 4) * 4 + (y + dy) % 4)

    def columns(index):
        return pl.ds(pl.multiple_of(index * slab, slab), slab)

    started = []

    def send(copy):
        copy.start()
        started.append(copy)

    def got(copy):
        copy.wait_recv()

    def here(index):
        locals_[index].wait()


    def finish():
        for copy in started:
            copy.wait_send()

    locals_ = [
        pltpu.make_async_copy(q_in.at[:, :, :, mine], qbuf.at[0, 0], local_sem.at[0]),
        pltpu.make_async_copy(k_in.at[:, mine], kbuf.at[0, 0], local_sem.at[1]),
        pltpu.make_async_copy(v_in.at[:, mine], vbuf.at[0, 0], local_sem.at[2]),
        pltpu.make_async_copy(w_in.at[:, columns(y)], wbuf.at[pl.ds(0, rows)], local_sem.at[3]),
        pltpu.make_async_copy(gate_in, gbuf, local_sem.at[4]),
        pltpu.make_async_copy(res_in, resbuf, local_sem.at[5]),
    ]
    for copy in locals_:
        copy.start()

    barrier = pltpu.get_barrier_semaphore()
    partners = [sib, par, crs] + [xpeer(dx) for dx in (1, 2, 3)]
    for partner in partners:
        pl.semaphore_signal(barrier, inc=1, device_id=partner, device_id_type=MESH)

    def greet(step, carry):
        pl.semaphore_signal(
            barrier, inc=1, device_id=tpeer(step // 4, step % 4), device_id_type=MESH
        )
        return carry

    lax.fori_loop(1, 16, greet, 0)
    pl.semaphore_wait(barrier, len(partners) + 15)

    q_cross = remote(q_in.at[:, :, :, other], qbuf.at[0, 1], (crs_sem.at[0, 0], crs_sem.at[1, 0]), crs)
    k_cross = remote(k_in.at[:, other], kbuf.at[2, 0], (crs_sem.at[0, 1], crs_sem.at[1, 1]), crs)
    v_cross = remote(v_in.at[:, other], vbuf.at[2, 0], (crs_sem.at[0, 2], crs_sem.at[1, 2]), crs)
    k_pair = remote(k_in.at[:, mine], kbuf.at[1, 0], (par_sem.at[0, 0], par_sem.at[1, 0]), par)
    v_pair = remote(v_in.at[:, mine], vbuf.at[1, 0], (par_sem.at[0, 1], par_sem.at[1, 1]), par)
    k_far = remote(kbuf.at[2, 0], kbuf.at[3, 0], (par_sem.at[0, 2], par_sem.at[1, 2]), par)
    v_far = remote(vbuf.at[2, 0], vbuf.at[3, 0], (par_sem.at[0, 3], par_sem.at[1, 3]), par)

    def share(buf, role, number):
        src = buf.at[role, 0]
        if role == 0:
            src = (k_in if number == 0 else v_in).at[:, mine]
        index = 2 * role + number
        return remote(src, buf.at[role, 1], (sib_sem.at[0, index], sib_sem.at[1, index]), sib)

    k_share = [share(kbuf, role, 0) for role in range(4)]
    v_share = [share(vbuf, role, 1) for role in range(4)]

    @functools.cache
    def q_across(part, dx):
        index = part * 3 + dx - 1
        src = q_in.at[:, :, :, mine] if part == 0 else qbuf.at[0, 1]
        return remote(
            src, qbuf.at[dx, part], (qx_sem.at[0, index], qx_sem.at[1, index]), xpeer(dx)
        )

    @functools.cache
    def w_send(dy):
        own_half = pl.ds(pl.multiple_of(half * core, half), half)
        there = pl.ds(pl.multiple_of(dy * rows + half * core, half), half)
        return remote(
            w_in.at[own_half, columns((y + dy) % 4)],
            wbuf.at[there],
            (w_sem.at[0, dy - 1], w_sem.at[1, dy - 1]),
            ypeer(dy),
        )

    @functools.cache
    def w_share(dy):
        there = pl.ds(pl.multiple_of(dy * rows + half * core, half), half)
        return remote(wbuf.at[there], wbuf.at[there], (wf_sem.at[0, dy - 1], wf_sem.at[1, dy - 1]), sib)

    send(k_pair)
    send(k_cross)
    send(v_pair)
    send(v_cross)
    send(q_cross)
    send(k_share[0])
    send(v_share[0])
    for dx in (1, 2, 3):
        send(q_across(0, dx))
    for dy in (1, 2, 3):
        send(w_send(dy))

    batch = 4 * rows

    def attend(role, spot):

        def load(ref):
            return ref[spot].reshape(batch, DH)

        k = kbuf[role].reshape(2 * rows, DH)
        v = vbuf[role].reshape(2 * rows, DH)
        count = 2 * rows // DH
        s = (
            lax.dot_general(load(qbuf), k, (((1,), (1,)), ((), ())), preferred_element_type=F32)
            * SCALE
        )
        m = jnp.broadcast_to(jnp.max(s, axis=1, keepdims=True), (batch, DH))
        if role > 0:
            before = load(peak)
            m = jnp.maximum(before, m)
            fade = jnp.exp2(before - m)
        p = jnp.exp2(s - jnp.concatenate([m] * count, axis=1))
        total = p[:, :DH]
        for part in range(1, count):
            total = total + p[:, part * DH : (part + 1) * DH]
        summed = jnp.dot(p.astype(BF16), v, preferred_element_type=F32)
        if role > 0:
            total = total + load(lsum) * fade
            summed = summed + load(acc) * fade
        return m, total, summed

    def attend_part(role, part):
        spot = (slice(None), part)
        m, total, summed = attend(role, spot)
        for ref, value in ((peak, m), (lsum, total), (acc, summed)):
            ref[spot] = value.reshape(ref[spot].shape)

    here(0)
    here(1)
    here(2)
    got(k_share[0])
    got(v_share[0])
    for dx in (1, 2, 3):
        got(q_across(0, dx))
    attend_part(0, 0)

    got(k_cross)
    send(k_far)
    send(k_share[2])
    got(k_pair)
    send(k_share[1])
    got(v_cross)
    send(v_far)
    send(v_share[2])
    got(v_pair)
    send(v_share[1])
    here(4)
    place = order_ref[x]
    level = noise_ref[0] * 0
    for slot in range(4):
        level = level + jnp.where(place == slot, noise_ref[slot], 0)
    levels = gbuf.shape[0]
    picker = (lax.broadcasted_iota(jnp.int32, (16, levels), 1) == level).astype(BF16)
    for piece in range(4):
        at = pl.ds(piece * slab, slab)
        gsel[:, at] = jnp.dot(picker, gbuf[:, at], preferred_element_type=F32)

    got(q_cross)
    for dx in (1, 2, 3):
        send(q_across(1, dx))
    got(k_share[1])
    got(v_share[1])
    attend_part(1, 0)
    got(k_share[2])
    got(v_share[2])
    attend_part(2, 0)
    for dx in (1, 2, 3):
        got(q_across(1, dx))
    attend_part(0, 1)
    got(k_far)
    send(k_share[3])
    attend_part(1, 1)
    got(v_far)
    send(v_share[3])
    attend_part(2, 1)
    got(k_share[3])
    got(v_share[3])

    @functools.cache
    def o_back(j, dx):
        index = j * 3 + dx - 1
        return remote(
            osend.at[j, dx],
            oret.at[j, dx - 1],
            (ox_sem.at[0, index], ox_sem.at[1, index]),
            xpeer(4 - dx),
        )

    @functools.cache
    def l_back(j, dx):
        index = j * 3 + dx - 1
        return remote(
            lsend.at[j, dx],
            lret.at[j, dx - 1],
            (lx_sem.at[0, index], lx_sem.at[1, index]),
            xpeer(4 - dx),
        )

    for j in (0, 1):
        m, total, summed = attend(3, (slice(None), slice(None), slice(None), j))
        total = jnp.sum(total, axis=1, keepdims=True)
        osend[j] = (summed * (1.0 / total)).astype(BF16).reshape(4, 2, half, DH)
        lse = m + jnp.log2(total)
        for dx in range(4):
            for part in (0, 1):
                first = (2 * dx + part) * half
                lsend[j, dx, part : part + 1] = lse[first : first + half].T[:1]
        for dx in (1, 2, 3):
            send(l_back(j, dx))
            send(o_back(j, dx))
        if j == 0:
            for dy in (1, 2, 3):
                got(w_send(dy))
                send(w_share(dy))


    seen = [order_ref[(x + dx) % 4] <= place for dx in (1, 2, 3)]

    def merged(j, part):
        states = [(lsend[j, 0, part : part + 1], osend[j, 0, part])]
        for dx in (1, 2, 3):
            lse = jnp.where(seen[dx - 1], lret[j, dx - 1, part : part + 1], NEG)
            states.append((lse, oret[j, dx - 1, part]))
        highest = states[0][0]
        for lse, _ in states[1:]:
            highest = jnp.maximum(highest, lse)
        shares = [jnp.exp2(lse - highest) for lse, _ in states]
        total = shares[0] + shares[1] + shares[2] + shares[3]
        result = jnp.zeros((half, DH), F32)
        for weight, (_, value) in zip(shares, states):
            result = result + jnp.broadcast_to(weight / total, (DH, DH)).T * value.astype(F32)
        return result.astype(BF16)

    def back(j):
        return remote(zsend.at[j], abuf.at[j, :, mine], (z_sem.at[0, j], z_sem.at[1, j]), crs)

    @functools.cache
    def a_send(j, which, dy):
        index = (2 * j + which) * 3 + dy - 1
        lane = head if which == 0 else 1 - head
        there = pl.ds(pl.multiple_of(dy * 2 * DH + lane * DH, DH), DH)
        return remote(
            abuf.at[j, :, mine if which == 0 else other],
            abuf.at[j, :, there],
            (a_sem.at[0, index], a_sem.at[1, index]),
            ypeer(dy),
        )

    backs = [back(0), back(1)]
    for j in (0, 1):
        for dx in (1, 2, 3):
            got(l_back(j, dx))
            got(o_back(j, dx))
        zsend[j] = merged(j, 1)
        send(backs[j])
        abuf[j, :, mine] = merged(j, 0)
        for dy in (1, 2, 3):
            send(a_send(j, 0, dy))
    for j in (0, 1):
        got(backs[j])
        for dy in (1, 2, 3):
            send(a_send(j, 1, dy))

    here(3)
    for dy in (1, 2, 3):
        got(w_share(dy))


    piece_width = 512

    def r_send(step):
        there = tpeer(step // 4, step % 4)
        to_y = there[1] % 4
        first = pl.ds(pl.multiple_of((there[1] // 4) * 32 + (to_y % 2) * 16, 16), 16)
        return remote(
            pbuf.at[to_y // 2, first],
            rbuf.at[step],
            (r_sem.at[0, step], r_sem.at[1, step]),
            there,
        )

    for j in (0, 1):
        for dy in (1, 2, 3):
            got(a_send(j, 0, dy))
            got(a_send(j, 1, dy))

        def project(i, carry):
            at = pl.ds(pl.multiple_of(i * piece_width, piece_width), piece_width)
            pbuf[j, :, at] = jnp.dot(abuf[j], wbuf[:, at], preferred_element_type=F32).astype(BF16)
            return carry

        lax.fori_loop(0, slab // piece_width, project, 0)

        def r_start(i, carry):
            dz = (i // 2 + 1) % 4
            step = dz * 4 + (2 * j + i % 2 + 4 - y) % 4

            @pl.when(step != 0)
            def _():
                r_send(step).start()

            return carry

        lax.fori_loop(0, 8, r_start, 0)

    own_rows = pl.ds(pl.multiple_of(zl * 32 + (y % 2) * 16, 16), 16)
    rbuf[0] = pbuf[y // 2, own_rows]

    here(5)
    for dy in (3, 2, 1, 0):
        at = columns((y + 4 - dy) % 4)
        for dz in range(4):
            if dz + dy > 0:
                r_send(4 * dz + dy).wait_recv()
        projected = rbuf[dy].astype(F32)
        for dz in (1, 2, 3):
            projected = projected + rbuf[4 * dz + dy].astype(F32)
        mixed = resbuf[:, at].astype(F32) + gsel[:, at] * projected
        out_ref[:, at] = mixed.astype(BF16)

    finish()

    def r_left(step, carry):
        r_send(step).wait_send()
        return carry

    lax.fori_loop(1, 16, r_left, 0)


def on_device(
    residual_in,
    query_rows,
    key_rows,
    value_rows,
    out_weight,
    gate_table,
    stretch_order,
    noise_levels,
):
    rows, width_in = query_rows.shape
    width = residual_in.shape[1]
    slab = width // 4
    any_spec = pl.BlockSpec(memory_space=pltpu.HBM)
    smem_spec = pl.BlockSpec(memory_space=pltpu.SMEM)
    dma = pltpu.SemaphoreType.DMA
    return pl.pallas_call(
        kernel,
        out_shape=jax.ShapeDtypeStruct(residual_in.shape, BF16),
        in_specs=[any_spec] * 6 + [smem_spec] * 2,
        out_specs=pl.BlockSpec(memory_space=pltpu.VMEM),
        scratch_shapes=[
            pltpu.VMEM((4, 2, 4, 2, rows // 8, DH), BF16),
            pltpu.VMEM((4, 2, rows, DH), BF16),
            pltpu.VMEM((4, 2, rows, DH), BF16),
            pltpu.VMEM((4, 2, 4, 2, rows // 8, DH), F32),
            pltpu.VMEM((4, 2, 4, 2, rows // 8, DH), F32),
            pltpu.VMEM((4, 2, 4, 2, rows // 8, DH), F32),
            pltpu.VMEM((2, 4, 2, rows // 2, DH), BF16),
            pltpu.VMEM((2, 4, 8, DH), F32),
            pltpu.VMEM((2, 3, 2, rows // 2, DH), BF16),
            pltpu.VMEM((2, 3, 8, DH), F32),
            pltpu.VMEM((2, rows // 2, DH), BF16),
            pltpu.VMEM((2, rows // 2, 8 * DH), BF16),
            pltpu.VMEM((4 * rows, slab), BF16),
            pltpu.VMEM((2, rows // 2, slab), BF16),
            pltpu.VMEM((16, 16, slab), BF16),
            pltpu.VMEM(gate_table.shape, BF16),
            pltpu.VMEM((16, width), F32),
            pltpu.VMEM(residual_in.shape, BF16),
            dma((6,)),
            dma((2, 8)),
            dma((2, 4)),
            dma((2, 3)),
            dma((2, 6)),
            dma((2, 6)),
            dma((2, 6)),
            dma((2, 2)),
            dma((2, 12)),
            dma((2, 3)),
            dma((2, 3)),
            dma((2, 16)),
        ],
        compiler_params=pltpu.CompilerParams(
            collective_id=0, has_side_effects=True, vmem_limit_bytes=62 * 1024 * 1024
        ),
        name="sublayer",
    )(
        residual_in,
        query_rows.reshape(4, 2, rows // 8, width_in),
        key_rows,
        value_rows,
        out_weight,
        gate_table,
        stretch_order,
        noise_levels,
    )


def solution(mesh):
    placed = (
        P(("ctx", "tp"), None),
        P("ctx", "tp"),
        P("ctx", "tp"),
        P("ctx", "tp"),
        P("tp", None),
        P(),
        P(),
        P(),
    )
    return jax.shard_map(
        on_device, mesh=mesh, in_specs=placed, out_specs=P(("ctx", "tp"), None), check_vma=False
    )
```

```python
import functools
import math

import jax
import jax.numpy as jnp
from jax import lax
from jax.experimental import pallas as pl
from jax.experimental.pallas import tpu as pltpu
from jax.sharding import PartitionSpec as P

MESH = pl.DeviceIdType.MESH
DH = 128
NEG = -1e30
BLOCKS = ((0, 1), (1, 2), (2, 4))
SCALE = math.log2(math.e) / math.sqrt(DH)
F32 = jnp.float32
BF16 = jnp.bfloat16


def remote(src, dst, sems, device):
    return pltpu.make_async_remote_copy(
        src_ref=src,
        dst_ref=dst,
        send_sem=sems[0],
        recv_sem=sems[1],
        device_id=device,
        device_id_type=MESH,
    )


def kernel(
    res_in,
    q_in,
    k_in,
    v_in,
    w_in,
    gate_in,
    order_ref,
    noise_ref,
    out_ref,
    qbuf,
    kbuf,
    vbuf,
    acc,
    lsum,
    peak,
    osend,
    lsend,
    oret,
    lret,
    zsend,
    abuf,
    wbuf,
    pbuf,
    rbuf,
    gbuf,
    gsel,
    resbuf,
    local_sem,
    sib_sem,
    par_sem,
    crs_sem,
    qx_sem,
    ox_sem,
    lx_sem,
    z_sem,
    a_sem,
    w_sem,
    wf_sem,
    r_sem,
):
    ctx = lax.axis_index("ctx")
    tp = lax.axis_index("tp")
    x = ctx // 8
    zh = (ctx // 2) % 4
    core = ctx % 2
    zl = tp // 4
    y = tp % 4
    odd = zl % 2
    ring = (zh + odd) % 4
    head = ring // 2
    mine = pl.ds(pl.multiple_of(head * DH, DH), DH)
    other = pl.ds(pl.multiple_of((1 - head) * DH, DH), DH)

    def at_ring(place):
        return (x * 8 + ((place + 4 - odd) % 4) * 2 + core, tp)

    sib = (ctx + 1 - 2 * core, tp)
    par = at_ring(ring + 1 - 2 * (ring % 2))
    crs = at_ring(3 - ring)
    rows = k_in.shape[0]
    half = rows // 2
    slab = wbuf.shape[1]

    def xpeer(dx):
        return (((x + dx) % 4) * 8 + zh * 2 + core, tp)

    def ypeer(dy):
        return (ctx, zl * 4 + (y + dy) % 4)

    def tpeer(dz, dy):
        return (ctx, ((zl + dz) % 4) * 4 + (y + dy) % 4)

    def columns(index):
        return pl.ds(pl.multiple_of(index * slab, slab), slab)

    started = []

    def send(copy):
        copy.start()
        started.append(copy)

    def got(copy):
        copy.wait_recv()

    def here(index):
        locals_[index].wait()


    def finish():
        for copy in started:
            copy.wait_send()

    locals_ = [
        pltpu.make_async_copy(q_in.at[:, :, :, mine], qbuf.at[0, 0], local_sem.at[0]),
        pltpu.make_async_copy(k_in.at[:, mine], kbuf.at[0, 0], local_sem.at[1]),
        pltpu.make_async_copy(v_in.at[:, mine], vbuf.at[0, 0], local_sem.at[2]),
        pltpu.make_async_copy(w_in.at[:, columns(y)], wbuf.at[pl.ds(0, rows)], local_sem.at[3]),
        pltpu.make_async_copy(gate_in, gbuf, local_sem.at[4]),
        pltpu.make_async_copy(res_in, resbuf, local_sem.at[5]),
    ]
    for copy in locals_:
        copy.start()

    barrier = pltpu.get_barrier_semaphore()
    partners = [sib, par, crs] + [xpeer(dx) for dx in (1, 2, 3)]
    for partner in partners:
        pl.semaphore_signal(barrier, inc=1, device_id=partner, device_id_type=MESH)

    def greet(step, carry):
        pl.semaphore_signal(
            barrier, inc=1, device_id=tpeer(step // 4, step % 4), device_id_type=MESH
        )
        return carry

    lax.fori_loop(1, 16, greet, 0)
    pl.semaphore_wait(barrier, len(partners) + 15)

    q_cross = remote(q_in.at[:, :, :, other], qbuf.at[0, 1], (crs_sem.at[0, 0], crs_sem.at[1, 0]), crs)
    k_cross = remote(k_in.at[:, other], kbuf.at[2, 0], (crs_sem.at[0, 1], crs_sem.at[1, 1]), crs)
    v_cross = remote(v_in.at[:, other], vbuf.at[2, 0], (crs_sem.at[0, 2], crs_sem.at[1, 2]), crs)
    k_pair = remote(k_in.at[:, mine], kbuf.at[1, 0], (par_sem.at[0, 0], par_sem.at[1, 0]), par)
    v_pair = remote(v_in.at[:, mine], vbuf.at[1, 0], (par_sem.at[0, 1], par_sem.at[1, 1]), par)
    k_far = remote(kbuf.at[2, 0], kbuf.at[3, 0], (par_sem.at[0, 2], par_sem.at[1, 2]), par)
    v_far = remote(vbuf.at[2, 0], vbuf.at[3, 0], (par_sem.at[0, 3], par_sem.at[1, 3]), par)

    def share(buf, role, number):
        src = buf.at[role, 0]
        if role == 0:
            src = (k_in if number == 0 else v_in).at[:, mine]
        index = 2 * role + number
        return remote(src, buf.at[role, 1], (sib_sem.at[0, index], sib_sem.at[1, index]), sib)

    k_share = [share(kbuf, role, 0) for role in range(4)]
    v_share = [share(vbuf, role, 1) for role in range(4)]

    @functools.cache
    def q_across(part, dx):
        index = part * 3 + dx - 1
        src = q_in.at[:, :, :, mine] if part == 0 else qbuf.at[0, 1]
        return remote(
            src, qbuf.at[dx, part], (qx_sem.at[0, index], qx_sem.at[1, index]), xpeer(dx)
        )

    @functools.cache
    def w_send(dy):
        own_half = pl.ds(pl.multiple_of(half * core, half), half)
        there = pl.ds(pl.multiple_of(dy * rows + half * core, half), half)
        return remote(
            w_in.at[own_half, columns((y + dy) % 4)],
            wbuf.at[there],
            (w_sem.at[0, dy - 1], w_sem.at[1, dy - 1]),
            ypeer(dy),
        )

    @functools.cache
    def w_share(dy):
        there = pl.ds(pl.multiple_of(dy * rows + half * core, half), half)
        return remote(wbuf.at[there], wbuf.at[there], (wf_sem.at[0, dy - 1], wf_sem.at[1, dy - 1]), sib)

    send(k_pair)
    send(k_cross)
    send(v_pair)
    send(v_cross)
    send(q_cross)
    send(k_share[0])
    send(v_share[0])
    for dx in (1, 2, 3):
        send(q_across(0, dx))
    for dy in (1, 2, 3):
        send(w_send(dy))

    def attend(role, spot, batch):

        def load(ref):
            return ref[spot].reshape(batch, DH)

        k = kbuf[role].reshape(2 * rows, DH)
        v = vbuf[role].reshape(2 * rows, DH)
        count = 2 * rows // DH
        s = (
            lax.dot_general(load(qbuf), k, (((1,), (1,)), ((), ())), preferred_element_type=F32)
            * SCALE
        )
        m = jnp.broadcast_to(jnp.max(s, axis=1, keepdims=True), (batch, DH))
        if role > 0:
            before = load(peak)
            m = jnp.maximum(before, m)
            fade = jnp.exp2(before - m)
        p = jnp.exp2(s - jnp.concatenate([m] * count, axis=1))
        total = p[:, :DH]
        for part in range(1, count):
            total = total + p[:, part * DH : (part + 1) * DH]
        summed = jnp.dot(p.astype(BF16), v, preferred_element_type=F32)
        if role > 0:
            total = total + load(lsum) * fade
            summed = summed + load(acc) * fade
        return m, total, summed

    def attend_part(role, part):
        spot = (slice(None), part)
        m, total, summed = attend(role, spot, 4 * rows)
        for ref, value in ((peak, m), (lsum, total), (acc, summed)):
            ref[spot] = value.reshape(ref[spot].shape)

    here(0)
    here(1)
    here(2)
    got(k_share[0])
    got(v_share[0])
    for dx in (1, 2, 3):
        got(q_across(0, dx))
    attend_part(0, 0)

    got(k_cross)
    send(k_far)
    send(k_share[2])
    got(k_pair)
    send(k_share[1])
    got(v_cross)
    send(v_far)
    send(v_share[2])
    got(v_pair)
    send(v_share[1])
    here(4)
    place = order_ref[x]
    level = noise_ref[0] * 0
    for slot in range(4):
        level = level + jnp.where(place == slot, noise_ref[slot], 0)
    levels = gbuf.shape[0]
    picker = (lax.broadcasted_iota(jnp.int32, (16, levels), 1) == level).astype(BF16)
    for piece in range(4):
        at = pl.ds(piece * slab, slab)
        gsel[:, at] = jnp.dot(picker, gbuf[:, at], preferred_element_type=F32)

    got(q_cross)
    for dx in (1, 2, 3):
        send(q_across(1, dx))
    got(k_share[1])
    got(v_share[1])
    attend_part(1, 0)
    got(k_share[2])
    got(v_share[2])
    attend_part(2, 0)
    for dx in (1, 2, 3):
        got(q_across(1, dx))
    attend_part(0, 1)
    got(k_far)
    send(k_share[3])
    attend_part(1, 1)
    got(v_far)
    send(v_share[3])
    attend_part(2, 1)
    got(k_share[3])
    got(v_share[3])

    def block_rows(j):
        first, past = BLOCKS[j]
        return pl.ds(first * rows // 4, (past - first) * rows // 4)

    @functools.cache
    def o_back(j, dx):
        index = j * 3 + dx - 1
        return remote(
            osend.at[dx, :, block_rows(j)],
            oret.at[dx - 1, :, block_rows(j)],
            (ox_sem.at[0, index], ox_sem.at[1, index]),
            xpeer(4 - dx),
        )

    @functools.cache
    def l_back(j, dx):
        index = j * 3 + dx - 1
        return remote(
            lsend.at[j, dx],
            lret.at[j, dx - 1],
            (lx_sem.at[0, index], lx_sem.at[1, index]),
            xpeer(4 - dx),
        )

    for j, (y_first, y_past) in enumerate(BLOCKS):
        count = y_past - y_first
        size = count * rows // 4
        m, total, summed = attend(
            3, (slice(None), slice(None), slice(None), slice(y_first, y_past)), 8 * size
        )
        total = jnp.sum(total, axis=1, keepdims=True)
        result = (summed * (1.0 / total)).astype(BF16).reshape(4, 2, 4, count, rows // 16, DH)
        lse = (m + jnp.log2(total)).reshape(8, size, DH)
        for dx in range(4):
            for part in (0, 1):
                for step in range(count):
                    there = pl.ds((y_first + step) * rows // 4, rows // 4)
                    osend[dx, part, there] = result[dx, part, :, step].reshape(rows // 4, DH)
                ordered = (
                    lse[2 * dx + part]
                    .reshape(4, count, rows // 16, DH)
                    .swapaxes(0, 1)
                    .reshape(size, DH)
                )
                lsend[j, dx, part : part + 1, :size] = ordered.T[:1]
        for dx in (1, 2, 3):
            send(l_back(j, dx))
            send(o_back(j, dx))
        if j == 0:
            for dy in (1, 2, 3):
                got(w_send(dy))
                send(w_share(dy))


    seen = [order_ref[(x + dx) % 4] <= place for dx in (1, 2, 3)]

    def merged(j, part):
        at = block_rows(j)
        size = at.size
        states = [(lsend[j, 0, part : part + 1, :size], osend[0, part, at])]
        for dx in (1, 2, 3):
            lse = jnp.where(seen[dx - 1], lret[j, dx - 1, part : part + 1, :size], NEG)
            states.append((lse, oret[dx - 1, part, at]))
        highest = states[0][0]
        for lse, _ in states[1:]:
            highest = jnp.maximum(highest, lse)
        shares = [jnp.exp2(lse - highest) for lse, _ in states]
        total = shares[0] + shares[1] + shares[2] + shares[3]
        result = jnp.zeros((size, DH), F32)
        for weight, (_, value) in zip(shares, states):
            result = result + jnp.broadcast_to(weight / total, (DH, size)).T * value.astype(F32)
        return result.astype(BF16)

    @functools.cache
    def back(j):
        at = block_rows(j)
        return remote(zsend.at[at], abuf.at[at, mine], (z_sem.at[0, j], z_sem.at[1, j]), crs)

    @functools.cache
    def a_send(j, which, dy):
        index = (2 * j + which) * 3 + dy - 1
        lane = head if which == 0 else 1 - head
        at = block_rows(j)
        there = pl.ds(pl.multiple_of(dy * 2 * DH + lane * DH, DH), DH)
        return remote(
            abuf.at[at, mine if which == 0 else other],
            abuf.at[at, there],
            (a_sem.at[0, index], a_sem.at[1, index]),
            ypeer(dy),
        )

    every = range(len(BLOCKS))
    for j in every:
        for dx in (1, 2, 3):
            got(l_back(j, dx))
            got(o_back(j, dx))
        zsend[block_rows(j)] = merged(j, 1)
        send(back(j))
        abuf[block_rows(j), mine] = merged(j, 0)
        for dy in (1, 2, 3):
            send(a_send(j, 0, dy))
    for j in every:
        got(back(j))
        for dy in (1, 2, 3):
            send(a_send(j, 1, dy))

    here(3)
    for dy in (1, 2, 3):
        got(w_share(dy))


    piece_width = 512

    def r_send(step):
        there = tpeer(step // 4, step % 4)
        first = pl.ds(pl.multiple_of((there[1] % 4) * 64 + (there[1] // 4) * 16, 16), 16)
        return remote(
            pbuf.at[first], rbuf.at[step], (r_sem.at[0, step], r_sem.at[1, step]), there
        )

    for j, (y_first, y_past) in enumerate(BLOCKS):
        for dy in (1, 2, 3):
            got(a_send(j, 0, dy))
            got(a_send(j, 1, dy))

        def project(i, carry):
            at = pl.ds(pl.multiple_of(i * piece_width, piece_width), piece_width)
            pbuf[block_rows(j), at] = jnp.dot(
                abuf[block_rows(j)], wbuf[:, at], preferred_element_type=F32
            ).astype(BF16)
            return carry

        lax.fori_loop(0, slab // piece_width, project, 0)

        count = y_past - y_first

        def r_start(i, carry):
            dz = (i // count + 1) % 4
            step = dz * 4 + (y_first + i % count + 4 - y) % 4

            @pl.when(step != 0)
            def _():
                r_send(step).start()

            return carry

        lax.fori_loop(0, 4 * count, r_start, 0)

    own_rows = pl.ds(pl.multiple_of(y * 64 + zl * 16, 16), 16)
    rbuf[0] = pbuf[own_rows]

    here(5)
    for dy in (3, 2, 1, 0):
        at = columns((y + 4 - dy) % 4)
        for dz in range(4):
            if dz + dy > 0:
                r_send(4 * dz + dy).wait_recv()
        projected = rbuf[dy].astype(F32)
        for dz in (1, 2, 3):
            projected = projected + rbuf[4 * dz + dy].astype(F32)
        mixed = resbuf[:, at].astype(F32) + gsel[:, at] * projected
        out_ref[:, at] = mixed.astype(BF16)

    finish()

    def r_left(step, carry):
        r_send(step).wait_send()
        return carry

    lax.fori_loop(1, 16, r_left, 0)


def on_device(
    residual_in,
    query_rows,
    key_rows,
    value_rows,
    out_weight,
    gate_table,
    stretch_order,
    noise_levels,
):
    rows, width_in = query_rows.shape
    width = residual_in.shape[1]
    slab = width // 4
    any_spec = pl.BlockSpec(memory_space=pltpu.HBM)
    smem_spec = pl.BlockSpec(memory_space=pltpu.SMEM)
    dma = pltpu.SemaphoreType.DMA
    return pl.pallas_call(
        kernel,
        out_shape=pltpu.VMEM(residual_in.shape, BF16),
        in_specs=[any_spec] * 6 + [smem_spec] * 2,
        out_specs=pl.BlockSpec(memory_space=pltpu.VMEM),
        scratch_shapes=[
            pltpu.VMEM((4, 2, 4, 4, rows // 16, DH), BF16),
            pltpu.VMEM((4, 2, rows, DH), BF16),
            pltpu.VMEM((4, 2, rows, DH), BF16),
            pltpu.VMEM((4, 2, 4, 4, rows // 16, DH), F32),
            pltpu.VMEM((4, 2, 4, 4, rows // 16, DH), F32),
            pltpu.VMEM((4, 2, 4, 4, rows // 16, DH), F32),
            pltpu.VMEM((4, 2, rows, DH), BF16),
            pltpu.VMEM((len(BLOCKS), 4, 8, DH), F32),
            pltpu.VMEM((3, 2, rows, DH), BF16),
            pltpu.VMEM((len(BLOCKS), 3, 8, DH), F32),
            pltpu.VMEM((rows, DH), BF16),
            pltpu.VMEM((rows, 8 * DH), BF16),
            pltpu.VMEM((4 * rows, slab), BF16),
            pltpu.VMEM((rows, slab), BF16),
            pltpu.VMEM((16, 16, slab), BF16),
            pltpu.VMEM(gate_table.shape, BF16),
            pltpu.VMEM((16, width), F32),
            pltpu.VMEM(residual_in.shape, BF16),
            dma((6,)),
            dma((2, 8)),
            dma((2, 4)),
            dma((2, 3)),
            dma((2, 6)),
            dma((2, 3 * len(BLOCKS))),
            dma((2, 3 * len(BLOCKS))),
            dma((2, len(BLOCKS))),
            dma((2, 6 * len(BLOCKS))),
            dma((2, 3)),
            dma((2, 3)),
            dma((2, 16)),
        ],
        compiler_params=pltpu.CompilerParams(
            collective_id=0, has_side_effects=True, vmem_limit_bytes=62 * 1024 * 1024
        ),
        name="sublayer",
    )(
        residual_in,
        query_rows.reshape(4, 4, rows // 16, width_in),
        key_rows,
        value_rows,
        out_weight,
        gate_table,
        stretch_order,
        noise_levels,
    )


def solution(mesh):
    placed = (
        P(("ctx", "tp"), None),
        P("ctx", "tp"),
        P("ctx", "tp"),
        P("ctx", "tp"),
        P("tp", None),
        P(),
        P(),
        P(),
    )
    return jax.shard_map(
        on_device, mesh=mesh, in_specs=placed, out_specs=P(("ctx", "tp"), None), check_vma=False
    )
```

```python
import functools
import math

import jax
import jax.numpy as jnp
from jax import lax
from jax.experimental import pallas as pl
from jax.experimental.pallas import tpu as pltpu
from jax.sharding import PartitionSpec as P

MESH = pl.DeviceIdType.MESH
DH = 128
NEG = -1e30
BLOCKS = ((0, 1), (1, 2), (2, 4))
PAIRED = (0,)
SCALE = math.log2(math.e) / math.sqrt(DH)
F32 = jnp.float32
BF16 = jnp.bfloat16


def remote(src, dst, sems, device):
    return pltpu.make_async_remote_copy(
        src_ref=src,
        dst_ref=dst,
        send_sem=sems[0],
        recv_sem=sems[1],
        device_id=device,
        device_id_type=MESH,
    )


def kernel(
    res_in,
    q_in,
    k_in,
    v_in,
    w_in,
    gate_in,
    order_ref,
    noise_ref,
    out_ref,
    qbuf,
    kbuf,
    vbuf,
    acc,
    lsum,
    peak,
    osend,
    lsend,
    oret,
    lret,
    zsend,
    abuf,
    wbuf,
    pbuf,
    rbuf,
    sbuf,
    gbuf,
    gsel,
    resbuf,
    local_sem,
    sib_sem,
    par_sem,
    crs_sem,
    qx_sem,
    ox_sem,
    lx_sem,
    z_sem,
    a_sem,
    w_sem,
    wf_sem,
    r_sem,
    s_sem,
):
    ctx = lax.axis_index("ctx")
    tp = lax.axis_index("tp")
    x = ctx // 8
    zh = (ctx // 2) % 4
    core = ctx % 2
    zl = tp // 4
    y = tp % 4
    odd = zl % 2
    ring = (zh + odd) % 4
    head = ring // 2
    mine = pl.ds(pl.multiple_of(head * DH, DH), DH)
    other = pl.ds(pl.multiple_of((1 - head) * DH, DH), DH)

    def at_ring(place):
        return (x * 8 + ((place + 4 - odd) % 4) * 2 + core, tp)

    sib = (ctx + 1 - 2 * core, tp)
    par = at_ring(ring + 1 - 2 * (ring % 2))
    crs = at_ring(3 - ring)
    rows = k_in.shape[0]
    half = rows // 2
    slab = wbuf.shape[1]

    def xpeer(dx):
        return (((x + dx) % 4) * 8 + zh * 2 + core, tp)

    def ypeer(dy):
        return (ctx, zl * 4 + (y + dy) % 4)

    def tpeer(dz, dy):
        return (ctx, ((zl + dz) % 4) * 4 + (y + dy) % 4)

    def columns(index):
        return pl.ds(pl.multiple_of(index * slab, slab), slab)

    started = []

    def send(copy):
        copy.start()
        started.append(copy)

    def got(copy):
        copy.wait_recv()

    def here(index):
        locals_[index].wait()


    def finish():
        for copy in started:
            copy.wait_send()

    locals_ = [
        pltpu.make_async_copy(q_in.at[:, :, :, mine], qbuf.at[0, 0], local_sem.at[0]),
        pltpu.make_async_copy(k_in.at[:, mine], kbuf.at[0, 0], local_sem.at[1]),
        pltpu.make_async_copy(v_in.at[:, mine], vbuf.at[0, 0], local_sem.at[2]),
        pltpu.make_async_copy(w_in.at[:, columns(y)], wbuf.at[pl.ds(0, rows)], local_sem.at[3]),
        pltpu.make_async_copy(gate_in, gbuf, local_sem.at[4]),
        pltpu.make_async_copy(res_in, resbuf, local_sem.at[5]),
    ]
    for copy in locals_:
        copy.start()

    barrier = pltpu.get_barrier_semaphore()
    partners = [sib, par, crs] + [xpeer(dx) for dx in (1, 2, 3)]
    for partner in partners:
        pl.semaphore_signal(barrier, inc=1, device_id=partner, device_id_type=MESH)

    def greet(step, carry):
        pl.semaphore_signal(
            barrier, inc=1, device_id=tpeer(step // 4, step % 4), device_id_type=MESH
        )
        return carry

    lax.fori_loop(1, 16, greet, 0)
    pl.semaphore_wait(barrier, len(partners) + 15)

    q_cross = remote(q_in.at[:, :, :, other], qbuf.at[0, 1], (crs_sem.at[0, 0], crs_sem.at[1, 0]), crs)
    k_cross = remote(k_in.at[:, other], kbuf.at[2, 0], (crs_sem.at[0, 1], crs_sem.at[1, 1]), crs)
    v_cross = remote(v_in.at[:, other], vbuf.at[2, 0], (crs_sem.at[0, 2], crs_sem.at[1, 2]), crs)
    k_pair = remote(k_in.at[:, mine], kbuf.at[1, 0], (par_sem.at[0, 0], par_sem.at[1, 0]), par)
    v_pair = remote(v_in.at[:, mine], vbuf.at[1, 0], (par_sem.at[0, 1], par_sem.at[1, 1]), par)
    k_far = remote(kbuf.at[2, 0], kbuf.at[3, 0], (par_sem.at[0, 2], par_sem.at[1, 2]), par)
    v_far = remote(vbuf.at[2, 0], vbuf.at[3, 0], (par_sem.at[0, 3], par_sem.at[1, 3]), par)

    def share(buf, role, number):
        src = buf.at[role, 0]
        if role == 0:
            src = (k_in if number == 0 else v_in).at[:, mine]
        index = 2 * role + number
        return remote(src, buf.at[role, 1], (sib_sem.at[0, index], sib_sem.at[1, index]), sib)

    k_share = [share(kbuf, role, 0) for role in range(4)]
    v_share = [share(vbuf, role, 1) for role in range(4)]

    @functools.cache
    def q_across(part, dx):
        index = part * 3 + dx - 1
        src = q_in.at[:, :, :, mine] if part == 0 else qbuf.at[0, 1]
        return remote(
            src, qbuf.at[dx, part], (qx_sem.at[0, index], qx_sem.at[1, index]), xpeer(dx)
        )

    @functools.cache
    def w_send(dy):
        own_half = pl.ds(pl.multiple_of(half * core, half), half)
        there = pl.ds(pl.multiple_of(dy * rows + half * core, half), half)
        return remote(
            w_in.at[own_half, columns((y + dy) % 4)],
            wbuf.at[there],
            (w_sem.at[0, dy - 1], w_sem.at[1, dy - 1]),
            ypeer(dy),
        )

    @functools.cache
    def w_share(dy):
        there = pl.ds(pl.multiple_of(dy * rows + half * core, half), half)
        return remote(wbuf.at[there], wbuf.at[there], (wf_sem.at[0, dy - 1], wf_sem.at[1, dy - 1]), sib)

    send(k_pair)
    send(k_cross)
    send(v_pair)
    send(v_cross)
    send(q_cross)
    send(k_share[0])
    send(v_share[0])
    for dx in (1, 2, 3):
        send(q_across(0, dx))
    for dy in (1, 2, 3):
        send(w_send(dy))

    def attend(role, spot, batch):

        def load(ref):
            return ref[spot].reshape(batch, DH)

        k = kbuf[role].reshape(2 * rows, DH)
        v = vbuf[role].reshape(2 * rows, DH)
        count = 2 * rows // DH
        s = (
            lax.dot_general(load(qbuf), k, (((1,), (1,)), ((), ())), preferred_element_type=F32)
            * SCALE
        )
        m = jnp.broadcast_to(jnp.max(s, axis=1, keepdims=True), (batch, DH))
        if role > 0:
            before = load(peak)
            m = jnp.maximum(before, m)
            fade = jnp.exp2(before - m)
        p = jnp.exp2(s - jnp.concatenate([m] * count, axis=1))
        total = p[:, :DH]
        for part in range(1, count):
            total = total + p[:, part * DH : (part + 1) * DH]
        summed = jnp.dot(p.astype(BF16), v, preferred_element_type=F32)
        if role > 0:
            total = total + load(lsum) * fade
            summed = summed + load(acc) * fade
        return m, total, summed

    def attend_part(role, part):
        spot = (slice(None), part)
        m, total, summed = attend(role, spot, 4 * rows)
        for ref, value in ((peak, m), (lsum, total), (acc, summed)):
            ref[spot] = value.reshape(ref[spot].shape)

    here(0)
    here(1)
    here(2)
    got(k_share[0])
    got(v_share[0])
    for dx in (1, 2, 3):
        got(q_across(0, dx))
    attend_part(0, 0)

    got(k_cross)
    send(k_far)
    send(k_share[2])
    got(k_pair)
    send(k_share[1])
    got(v_cross)
    send(v_far)
    send(v_share[2])
    got(v_pair)
    send(v_share[1])
    here(4)
    place = order_ref[x]
    level = noise_ref[0] * 0
    for slot in range(4):
        level = level + jnp.where(place == slot, noise_ref[slot], 0)
    levels = gbuf.shape[0]
    picker = (lax.broadcasted_iota(jnp.int32, (16, levels), 1) == level).astype(BF16)
    for piece in range(4):
        at = pl.ds(piece * slab, slab)
        gsel[:, at] = jnp.dot(picker, gbuf[:, at], preferred_element_type=F32)

    got(q_cross)
    for dx in (1, 2, 3):
        send(q_across(1, dx))
    got(k_share[1])
    got(v_share[1])
    attend_part(1, 0)
    got(k_share[2])
    got(v_share[2])
    attend_part(2, 0)
    for dx in (1, 2, 3):
        got(q_across(1, dx))
    attend_part(0, 1)
    got(k_far)
    send(k_share[3])
    attend_part(1, 1)
    got(v_far)
    send(v_share[3])
    attend_part(2, 1)
    got(k_share[3])
    got(v_share[3])

    def block_rows(j):
        first, past = BLOCKS[j]
        return pl.ds(first * rows // 4, (past - first) * rows // 4)

    @functools.cache
    def o_back(j, dx):
        index = j * 3 + dx - 1
        return remote(
            osend.at[dx, :, block_rows(j)],
            oret.at[dx - 1, :, block_rows(j)],
            (ox_sem.at[0, index], ox_sem.at[1, index]),
            xpeer(4 - dx),
        )

    @functools.cache
    def l_back(j, dx):
        index = j * 3 + dx - 1
        return remote(
            lsend.at[j, dx],
            lret.at[j, dx - 1],
            (lx_sem.at[0, index], lx_sem.at[1, index]),
            xpeer(4 - dx),
        )

    for j, (y_first, y_past) in enumerate(BLOCKS):
        count = y_past - y_first
        size = count * rows // 4
        m, total, summed = attend(
            3, (slice(None), slice(None), slice(None), slice(y_first, y_past)), 8 * size
        )
        total = jnp.sum(total, axis=1, keepdims=True)
        result = (summed * (1.0 / total)).astype(BF16).reshape(4, 2, 4, count, rows // 16, DH)
        lse = (m + jnp.log2(total)).reshape(8, size, DH)
        for dx in range(4):
            for part in (0, 1):
                for step in range(count):
                    there = pl.ds((y_first + step) * rows // 4, rows // 4)
                    osend[dx, part, there] = result[dx, part, :, step].reshape(rows // 4, DH)
                ordered = (
                    lse[2 * dx + part]
                    .reshape(4, count, rows // 16, DH)
                    .swapaxes(0, 1)
                    .reshape(size, DH)
                )
                lsend[j, dx, part : part + 1, :size] = ordered.T[:1]
        for dx in (1, 2, 3):
            send(l_back(j, dx))
            send(o_back(j, dx))
        if j == 0:
            for dy in (1, 2, 3):
                got(w_send(dy))
                send(w_share(dy))


    seen = [order_ref[(x + dx) % 4] <= place for dx in (1, 2, 3)]

    def merged(j, part):
        at = block_rows(j)
        size = at.size
        states = [(lsend[j, 0, part : part + 1, :size], osend[0, part, at])]
        for dx in (1, 2, 3):
            lse = jnp.where(seen[dx - 1], lret[j, dx - 1, part : part + 1, :size], NEG)
            states.append((lse, oret[dx - 1, part, at]))
        highest = states[0][0]
        for lse, _ in states[1:]:
            highest = jnp.maximum(highest, lse)
        shares = [jnp.exp2(lse - highest) for lse, _ in states]
        total = shares[0] + shares[1] + shares[2] + shares[3]
        result = jnp.zeros((size, DH), F32)
        for weight, (_, value) in zip(shares, states):
            result = result + jnp.broadcast_to(weight / total, (DH, size)).T * value.astype(F32)
        return result.astype(BF16)

    @functools.cache
    def back(j):
        at = block_rows(j)
        return remote(zsend.at[at], abuf.at[at, mine], (z_sem.at[0, j], z_sem.at[1, j]), crs)

    @functools.cache
    def a_send(j, which, dy):
        index = (2 * j + which) * 3 + dy - 1
        lane = head if which == 0 else 1 - head
        at = block_rows(j)
        there = pl.ds(pl.multiple_of(dy * 2 * DH + lane * DH, DH), DH)
        return remote(
            abuf.at[at, mine if which == 0 else other],
            abuf.at[at, there],
            (a_sem.at[0, index], a_sem.at[1, index]),
            ypeer(dy),
        )

    every = range(len(BLOCKS))
    for j in every:
        for dx in (1, 2, 3):
            got(l_back(j, dx))
            got(o_back(j, dx))
        zsend[block_rows(j)] = merged(j, 1)
        send(back(j))
        abuf[block_rows(j), mine] = merged(j, 0)
        for dy in (1, 2, 3):
            send(a_send(j, 0, dy))
    for j in every:
        got(back(j))
        for dy in (1, 2, 3):
            send(a_send(j, 1, dy))

    here(3)
    for dy in (1, 2, 3):
        got(w_share(dy))


    piece_width = 512

    def r_send(step):
        there = tpeer(step // 4, step % 4)
        first = pl.ds(pl.multiple_of((there[1] % 4) * 64 + (there[1] // 4) * 16, 16), 16)
        return remote(
            pbuf.at[first], rbuf.at[step], (r_sem.at[0, step], r_sem.at[1, step]), there
        )

    outer = zl % 3 == 0
    buddy = (ctx, (zl + 1 - 2 * (zl % 2)) * 4 + y)

    def paired(to_y):
        result = to_y == PAIRED[0]
        for value in PAIRED[1:]:
            result = jnp.logical_or(result, to_y == value)
        return result

    def across(other_zl):
        return other_zl // 2 != zl // 2

    def pair_rows(n):
        return pl.ds(pl.multiple_of(PAIRED[n] * 64 + 32 * (1 - zl // 2), 32), 32)

    def pair_send(n):
        return remote(pbuf.at[pair_rows(n)], sbuf.at[n], (s_sem.at[0, n], s_sem.at[1, n]), buddy)

    for j, (y_first, y_past) in enumerate(BLOCKS):
        for dy in (1, 2, 3):
            got(a_send(j, 0, dy))
            got(a_send(j, 1, dy))

        def project(i, carry):
            at = pl.ds(pl.multiple_of(i * piece_width, piece_width), piece_width)
            pbuf[block_rows(j), at] = jnp.dot(
                abuf[block_rows(j)], wbuf[:, at], preferred_element_type=F32
            ).astype(BF16)
            return carry

        lax.fori_loop(0, slab // piece_width, project, 0)

        for n, to_y in enumerate(PAIRED):
            if y_first <= to_y < y_past:
                pl.when(outer)(pair_send(n).start)

        count = y_past - y_first

        def r_start(i, carry):
            dz = (i // count + 1) % 4
            to_y = y_first + i % count
            step = dz * 4 + (to_y + 4 - y) % 4
            later = jnp.logical_and(paired(to_y), across((zl + dz) % 4))

            @pl.when(jnp.logical_and(step != 0, jnp.logical_not(later)))
            def _():
                r_send(step).start()

            return carry

        lax.fori_loop(0, 4 * count, r_start, 0)

    for n, to_y in enumerate(PAIRED):

        @pl.when(jnp.logical_not(outer))
        def _():
            pair_send(n).wait_recv()
            at = pair_rows(n)
            pbuf[at] = (pbuf[at].astype(F32) + sbuf[n].astype(F32)).astype(BF16)
            for which in (0, 1):
                to_zl = 2 * (1 - zl // 2) + which
                r_send((to_zl + 4 - zl) % 4 * 4 + (to_y + 4 - y) % 4).start()

    own_rows = pl.ds(pl.multiple_of(y * 64 + zl * 16, 16), 16)
    rbuf[0] = pbuf[own_rows]

    here(5)
    absent = []
    for dz in range(4):
        from_zl = (zl + 4 - dz) % 4
        absent.append(
            jnp.logical_and(paired(y), jnp.logical_and(across(from_zl), from_zl % 3 == 0))
        )
    for dy in (3, 2, 1, 0):
        at = columns((y + 4 - dy) % 4)
        for dz in range(4):
            if dz + dy > 0:
                pl.when(jnp.logical_not(absent[dz]))(r_send(4 * dz + dy).wait_recv)
        projected = rbuf[dy].astype(F32)
        for dz in (1, 2, 3):
            part = rbuf[4 * dz + dy].astype(F32)
            projected = projected + jnp.where(absent[dz], 0.0, part)
        mixed = resbuf[:, at].astype(F32) + gsel[:, at] * projected
        out_ref[:, at] = mixed.astype(BF16)

    finish()

    def r_left(step, carry):
        held = jnp.logical_and(paired((y + step) % 4), across((zl + step // 4) % 4))

        @pl.when(jnp.logical_not(jnp.logical_and(held, outer)))
        def _():
            r_send(step).wait_send()

        return carry

    lax.fori_loop(1, 16, r_left, 0)
    for n in range(len(PAIRED)):
        pl.when(outer)(pair_send(n).wait_send)


def on_device(
    residual_in,
    query_rows,
    key_rows,
    value_rows,
    out_weight,
    gate_table,
    stretch_order,
    noise_levels,
):
    rows, width_in = query_rows.shape
    width = residual_in.shape[1]
    slab = width // 4
    any_spec = pl.BlockSpec(memory_space=pltpu.HBM)
    smem_spec = pl.BlockSpec(memory_space=pltpu.SMEM)
    dma = pltpu.SemaphoreType.DMA
    return pl.pallas_call(
        kernel,
        out_shape=pltpu.VMEM(residual_in.shape, BF16),
        in_specs=[any_spec] * 6 + [smem_spec] * 2,
        out_specs=pl.BlockSpec(memory_space=pltpu.VMEM),
        scratch_shapes=[
            pltpu.VMEM((4, 2, 4, 4, rows // 16, DH), BF16),
            pltpu.VMEM((4, 2, rows, DH), BF16),
            pltpu.VMEM((4, 2, rows, DH), BF16),
            pltpu.VMEM((4, 2, 4, 4, rows // 16, DH), F32),
            pltpu.VMEM((4, 2, 4, 4, rows // 16, DH), F32),
            pltpu.VMEM((4, 2, 4, 4, rows // 16, DH), F32),
            pltpu.VMEM((4, 2, rows, DH), BF16),
            pltpu.VMEM((len(BLOCKS), 4, 8, DH), F32),
            pltpu.VMEM((3, 2, rows, DH), BF16),
            pltpu.VMEM((len(BLOCKS), 3, 8, DH), F32),
            pltpu.VMEM((rows, DH), BF16),
            pltpu.VMEM((rows, 8 * DH), BF16),
            pltpu.VMEM((4 * rows, slab), BF16),
            pltpu.VMEM((rows, slab), BF16),
            pltpu.VMEM((16, 16, slab), BF16),
            pltpu.VMEM((len(PAIRED), 32, slab), BF16),
            pltpu.VMEM(gate_table.shape, BF16),
            pltpu.VMEM((16, width), F32),
            pltpu.VMEM(residual_in.shape, BF16),
            dma((6,)),
            dma((2, 8)),
            dma((2, 4)),
            dma((2, 3)),
            dma((2, 6)),
            dma((2, 3 * len(BLOCKS))),
            dma((2, 3 * len(BLOCKS))),
            dma((2, len(BLOCKS))),
            dma((2, 6 * len(BLOCKS))),
            dma((2, 3)),
            dma((2, 3)),
            dma((2, 16)),
            dma((2, len(PAIRED))),
        ],
        compiler_params=pltpu.CompilerParams(
            collective_id=0, has_side_effects=True, vmem_limit_bytes=62 * 1024 * 1024
        ),
        name="sublayer",
    )(
        residual_in,
        query_rows.reshape(4, 4, rows // 16, width_in),
        key_rows,
        value_rows,
        out_weight,
        gate_table,
        stretch_order,
        noise_levels,
    )


def solution(mesh):
    placed = (
        P(("ctx", "tp"), None),
        P("ctx", "tp"),
        P("ctx", "tp"),
        P("ctx", "tp"),
        P("tp", None),
        P(),
        P(),
        P(),
    )
    return jax.shard_map(
        on_device, mesh=mesh, in_specs=placed, out_specs=P(("ctx", "tp"), None), check_vma=False
    )
```

```python
import functools
import math

import jax
import jax.numpy as jnp
from jax import lax
from jax.experimental import pallas as pl
from jax.experimental.pallas import tpu as pltpu
from jax.sharding import PartitionSpec as P

MESH = pl.DeviceIdType.MESH
DH = 128
NEG = -1e30
BLOCKS = ((0, 1), (1, 3), (3, 4))
PAIRED = (0,)
SCALE = math.log2(math.e) / math.sqrt(DH)
F32 = jnp.float32
BF16 = jnp.bfloat16


def remote(src, dst, sems, device):
    return pltpu.make_async_remote_copy(
        src_ref=src,
        dst_ref=dst,
        send_sem=sems[0],
        recv_sem=sems[1],
        device_id=device,
        device_id_type=MESH,
    )


def kernel(
    res_in,
    q_in,
    k_in,
    v_in,
    w_in,
    gate_in,
    order_ref,
    noise_ref,
    out_ref,
    qbuf,
    kbuf,
    vbuf,
    acc,
    lsum,
    peak,
    osend,
    lsend,
    oret,
    lret,
    zsend,
    abuf,
    wbuf,
    pbuf,
    rbuf,
    sbuf,
    gbuf,
    gsel,
    resbuf,
    local_sem,
    sib_sem,
    par_sem,
    crs_sem,
    qx_sem,
    ox_sem,
    lx_sem,
    z_sem,
    a_sem,
    w_sem,
    wf_sem,
    r_sem,
    s_sem,
):
    ctx = lax.axis_index("ctx")
    tp = lax.axis_index("tp")
    x = ctx // 8
    zh = (ctx // 2) % 4
    core = ctx % 2
    zl = tp // 4
    y = tp % 4
    odd = zl % 2
    ring = (zh + odd) % 4
    head = ring // 2
    mine = pl.ds(pl.multiple_of(head * DH, DH), DH)
    other = pl.ds(pl.multiple_of((1 - head) * DH, DH), DH)

    def at_ring(place):
        return (x * 8 + ((place + 4 - odd) % 4) * 2 + core, tp)

    sib = (ctx + 1 - 2 * core, tp)
    par = at_ring(ring + 1 - 2 * (ring % 2))
    crs = at_ring(3 - ring)
    rows = k_in.shape[0]
    half = rows // 2
    slab = wbuf.shape[1]

    def xpeer(dx):
        return (((x + dx) % 4) * 8 + zh * 2 + core, tp)

    def ypeer(dy):
        return (ctx, zl * 4 + (y + dy) % 4)

    def tpeer(dz, dy):
        return (ctx, ((zl + dz) % 4) * 4 + (y + dy) % 4)

    def columns(index):
        return pl.ds(pl.multiple_of(index * slab, slab), slab)

    started = []

    def send(copy):
        copy.start()
        started.append(copy)

    def got(copy):
        copy.wait_recv()

    def here(index):
        locals_[index].wait()


    def finish():
        for copy in started:
            copy.wait_send()

    locals_ = [
        pltpu.make_async_copy(q_in.at[:, :, :, mine], qbuf.at[0, 0], local_sem.at[0]),
        pltpu.make_async_copy(k_in.at[:, mine], kbuf.at[0, 0], local_sem.at[1]),
        pltpu.make_async_copy(v_in.at[:, mine], vbuf.at[0, 0], local_sem.at[2]),
        pltpu.make_async_copy(w_in.at[:, columns(y)], wbuf.at[pl.ds(0, rows)], local_sem.at[3]),
        pltpu.make_async_copy(gate_in, gbuf, local_sem.at[4]),
        pltpu.make_async_copy(res_in, resbuf, local_sem.at[5]),
    ]
    for copy in locals_:
        copy.start()

    barrier = pltpu.get_barrier_semaphore()
    partners = [sib, par, crs] + [xpeer(dx) for dx in (1, 2, 3)]
    for partner in partners:
        pl.semaphore_signal(barrier, inc=1, device_id=partner, device_id_type=MESH)

    def greet(step, carry):
        pl.semaphore_signal(
            barrier, inc=1, device_id=tpeer(step // 4, step % 4), device_id_type=MESH
        )
        return carry

    lax.fori_loop(1, 16, greet, 0)
    pl.semaphore_wait(barrier, len(partners) + 15)

    q_cross = remote(q_in.at[:, :, :, other], qbuf.at[0, 1], (crs_sem.at[0, 0], crs_sem.at[1, 0]), crs)
    k_cross = remote(k_in.at[:, other], kbuf.at[2, 0], (crs_sem.at[0, 1], crs_sem.at[1, 1]), crs)
    v_cross = remote(v_in.at[:, other], vbuf.at[2, 0], (crs_sem.at[0, 2], crs_sem.at[1, 2]), crs)
    k_pair = remote(k_in.at[:, mine], kbuf.at[1, 0], (par_sem.at[0, 0], par_sem.at[1, 0]), par)
    v_pair = remote(v_in.at[:, mine], vbuf.at[1, 0], (par_sem.at[0, 1], par_sem.at[1, 1]), par)
    k_far = remote(kbuf.at[2, 0], kbuf.at[3, 0], (par_sem.at[0, 2], par_sem.at[1, 2]), par)
    v_far = remote(vbuf.at[2, 0], vbuf.at[3, 0], (par_sem.at[0, 3], par_sem.at[1, 3]), par)

    def share(buf, role, number):
        src = buf.at[role, 0]
        if role == 0:
            src = (k_in if number == 0 else v_in).at[:, mine]
        index = 2 * role + number
        return remote(src, buf.at[role, 1], (sib_sem.at[0, index], sib_sem.at[1, index]), sib)

    k_share = [share(kbuf, role, 0) for role in range(4)]
    v_share = [share(vbuf, role, 1) for role in range(4)]

    @functools.cache
    def q_across(part, dx):
        index = part * 3 + dx - 1
        src = q_in.at[:, :, :, mine] if part == 0 else qbuf.at[0, 1]
        return remote(
            src, qbuf.at[dx, part], (qx_sem.at[0, index], qx_sem.at[1, index]), xpeer(dx)
        )

    @functools.cache
    def w_send(dy):
        own_half = pl.ds(pl.multiple_of(half * core, half), half)
        there = pl.ds(pl.multiple_of(dy * rows + half * core, half), half)
        return remote(
            w_in.at[own_half, columns((y + dy) % 4)],
            wbuf.at[there],
            (w_sem.at[0, dy - 1], w_sem.at[1, dy - 1]),
            ypeer(dy),
        )

    @functools.cache
    def w_share(dy):
        there = pl.ds(pl.multiple_of(dy * rows + half * core, half), half)
        return remote(wbuf.at[there], wbuf.at[there], (wf_sem.at[0, dy - 1], wf_sem.at[1, dy - 1]), sib)

    send(k_pair)
    send(k_cross)
    send(v_pair)
    send(v_cross)
    send(q_cross)
    send(k_share[0])
    send(v_share[0])
    for dx in (1, 2, 3):
        send(q_across(0, dx))
    for dy in (1, 2, 3):
        send(w_send(dy))

    def attend(role, spot, batch):

        def load(ref):
            return ref[spot].reshape(batch, DH)

        k = kbuf[role].reshape(2 * rows, DH)
        v = vbuf[role].reshape(2 * rows, DH)
        count = 2 * rows // DH
        s = (
            lax.dot_general(load(qbuf), k, (((1,), (1,)), ((), ())), preferred_element_type=F32)
            * SCALE
        )
        m = jnp.broadcast_to(jnp.max(s, axis=1, keepdims=True), (batch, DH))
        if role > 0:
            before = load(peak)
            m = jnp.maximum(before, m)
            fade = jnp.exp2(before - m)
        p = jnp.exp2(s - jnp.concatenate([m] * count, axis=1))
        total = p[:, :DH]
        for part in range(1, count):
            total = total + p[:, part * DH : (part + 1) * DH]
        summed = jnp.dot(p.astype(BF16), v, preferred_element_type=F32)
        if role > 0:
            total = total + load(lsum) * fade
            summed = summed + load(acc) * fade
        return m, total, summed

    def attend_part(role, part):
        spot = (slice(None), part)
        m, total, summed = attend(role, spot, 4 * rows)
        for ref, value in ((peak, m), (lsum, total), (acc, summed)):
            ref[spot] = value.reshape(ref[spot].shape)

    here(0)
    here(1)
    here(2)
    got(k_share[0])
    got(v_share[0])
    for dx in (1, 2, 3):
        got(q_across(0, dx))
    attend_part(0, 0)

    got(k_cross)
    send(k_far)
    send(k_share[2])
    got(k_pair)
    send(k_share[1])
    got(v_cross)
    send(v_far)
    send(v_share[2])
    got(v_pair)
    send(v_share[1])
    here(4)
    place = order_ref[x]
    level = noise_ref[0] * 0
    for slot in range(4):
        level = level + jnp.where(place == slot, noise_ref[slot], 0)
    levels = gbuf.shape[0]
    picker = (lax.broadcasted_iota(jnp.int32, (16, levels), 1) == level).astype(BF16)
    for piece in range(4):
        at = pl.ds(piece * slab, slab)
        gsel[:, at] = jnp.dot(picker, gbuf[:, at], preferred_element_type=F32)

    got(q_cross)
    for dx in (1, 2, 3):
        send(q_across(1, dx))
    got(k_share[1])
    got(v_share[1])
    attend_part(1, 0)
    got(k_share[2])
    got(v_share[2])
    attend_part(2, 0)
    for dx in (1, 2, 3):
        got(q_across(1, dx))
    attend_part(0, 1)
    got(k_far)
    send(k_share[3])
    attend_part(1, 1)
    got(v_far)
    send(v_share[3])
    attend_part(2, 1)
    got(k_share[3])
    got(v_share[3])

    def block_rows(j):
        first, past = BLOCKS[j]
        return pl.ds(first * rows // 4, (past - first) * rows // 4)

    @functools.cache
    def o_back(j, dx):
        index = j * 3 + dx - 1
        return remote(
            osend.at[dx, :, block_rows(j)],
            oret.at[dx - 1, :, block_rows(j)],
            (ox_sem.at[0, index], ox_sem.at[1, index]),
            xpeer(4 - dx),
        )

    @functools.cache
    def l_back(j, dx):
        index = j * 3 + dx - 1
        return remote(
            lsend.at[j, dx],
            lret.at[j, dx - 1],
            (lx_sem.at[0, index], lx_sem.at[1, index]),
            xpeer(4 - dx),
        )

    for j, (y_first, y_past) in enumerate(BLOCKS):
        count = y_past - y_first
        size = count * rows // 4
        m, total, summed = attend(
            3, (slice(None), slice(None), slice(None), slice(y_first, y_past)), 8 * size
        )
        total = jnp.sum(total, axis=1, keepdims=True)
        result = (summed * (1.0 / total)).astype(BF16).reshape(4, 2, 4, count, rows // 16, DH)
        lse = (m + jnp.log2(total)).reshape(8, size, DH)
        for dx in range(4):
            for part in (0, 1):
                for step in range(count):
                    there = pl.ds((y_first + step) * rows // 4, rows // 4)
                    osend[dx, part, there] = result[dx, part, :, step].reshape(rows // 4, DH)
                ordered = (
                    lse[2 * dx + part]
                    .reshape(4, count, rows // 16, DH)
                    .swapaxes(0, 1)
                    .reshape(size, DH)
                )
                lsend[j, dx, part : part + 1, :size] = ordered.T[:1]
        for dx in (1, 2, 3):
            send(l_back(j, dx))
            send(o_back(j, dx))
        if j == 0:
            for dy in (1, 2, 3):
                got(w_send(dy))
                send(w_share(dy))


    seen = [order_ref[(x + dx) % 4] <= place for dx in (1, 2, 3)]

    def merged(j, part):
        at = block_rows(j)
        size = at.size
        states = [(lsend[j, 0, part : part + 1, :size], osend[0, part, at])]
        for dx in (1, 2, 3):
            lse = jnp.where(seen[dx - 1], lret[j, dx - 1, part : part + 1, :size], NEG)
            states.append((lse, oret[dx - 1, part, at]))
        highest = states[0][0]
        for lse, _ in states[1:]:
            highest = jnp.maximum(highest, lse)
        shares = [jnp.exp2(lse - highest) for lse, _ in states]
        total = shares[0] + shares[1] + shares[2] + shares[3]
        result = jnp.zeros((size, DH), F32)
        for weight, (_, value) in zip(shares, states):
            result = result + jnp.broadcast_to(weight / total, (DH, size)).T * value.astype(F32)
        return result.astype(BF16)

    @functools.cache
    def back(j):
        at = block_rows(j)
        return remote(zsend.at[at], abuf.at[at, mine], (z_sem.at[0, j], z_sem.at[1, j]), crs)

    @functools.cache
    def a_send(j, which, dy):
        index = (2 * j + which) * 3 + dy - 1
        lane = head if which == 0 else 1 - head
        at = block_rows(j)
        there = pl.ds(pl.multiple_of(dy * 2 * DH + lane * DH, DH), DH)
        return remote(
            abuf.at[at, mine if which == 0 else other],
            abuf.at[at, there],
            (a_sem.at[0, index], a_sem.at[1, index]),
            ypeer(dy),
        )

    every = range(len(BLOCKS))
    for j in every:
        for dx in (1, 2, 3):
            got(l_back(j, dx))
            got(o_back(j, dx))
        zsend[block_rows(j)] = merged(j, 1)
        send(back(j))
        abuf[block_rows(j), mine] = merged(j, 0)
        for dy in (1, 2, 3):
            send(a_send(j, 0, dy))
    for j in every:
        got(back(j))
        for dy in (1, 2, 3):
            send(a_send(j, 1, dy))

    here(3)
    for dy in (1, 2, 3):
        got(w_share(dy))


    piece_width = 512

    def r_send(step):
        there = tpeer(step // 4, step % 4)
        first = pl.ds(pl.multiple_of((there[1] % 4) * 64 + (there[1] // 4) * 16, 16), 16)
        return remote(
            pbuf.at[first], rbuf.at[step], (r_sem.at[0, step], r_sem.at[1, step]), there
        )

    outer = zl % 3 == 0
    buddy = (ctx, (zl + 1 - 2 * (zl % 2)) * 4 + y)

    def paired(to_y):
        result = to_y == PAIRED[0]
        for value in PAIRED[1:]:
            result = jnp.logical_or(result, to_y == value)
        return result

    def across(other_zl):
        return other_zl // 2 != zl // 2

    def pair_rows(n):
        return pl.ds(pl.multiple_of(PAIRED[n] * 64 + 32 * (1 - zl // 2), 32), 32)

    def pair_send(n):
        return remote(pbuf.at[pair_rows(n)], sbuf.at[n], (s_sem.at[0, n], s_sem.at[1, n]), buddy)

    for j, (y_first, y_past) in enumerate(BLOCKS):
        for dy in (1, 2, 3):
            got(a_send(j, 0, dy))
            got(a_send(j, 1, dy))

        def project(i, carry):
            at = pl.ds(pl.multiple_of(i * piece_width, piece_width), piece_width)
            pbuf[block_rows(j), at] = jnp.dot(
                abuf[block_rows(j)], wbuf[:, at], preferred_element_type=F32
            ).astype(BF16)
            return carry

        lax.fori_loop(0, slab // piece_width, project, 0)

        for n, to_y in enumerate(PAIRED):
            if y_first <= to_y < y_past:
                pl.when(outer)(pair_send(n).start)

        count = y_past - y_first

        def r_start(i, carry):
            dz = (i // count + 1) % 4
            to_y = y_first + i % count
            step = dz * 4 + (to_y + 4 - y) % 4
            later = jnp.logical_and(paired(to_y), across((zl + dz) % 4))

            @pl.when(jnp.logical_and(step != 0, jnp.logical_not(later)))
            def _():
                r_send(step).start()

            return carry

        lax.fori_loop(0, 4 * count, r_start, 0)

    for n, to_y in enumerate(PAIRED):

        @pl.when(jnp.logical_not(outer))
        def _():
            pair_send(n).wait_recv()
            at = pair_rows(n)
            pbuf[at] = (pbuf[at].astype(F32) + sbuf[n].astype(F32)).astype(BF16)
            for which in (0, 1):
                to_zl = 2 * (1 - zl // 2) + which
                r_send((to_zl + 4 - zl) % 4 * 4 + (to_y + 4 - y) % 4).start()

    own_rows = pl.ds(pl.multiple_of(y * 64 + zl * 16, 16), 16)
    rbuf[0] = pbuf[own_rows]

    here(5)
    absent = []
    for dz in range(4):
        from_zl = (zl + 4 - dz) % 4
        absent.append(
            jnp.logical_and(paired(y), jnp.logical_and(across(from_zl), from_zl % 3 == 0))
        )
    for dy in (3, 2, 1, 0):
        at = columns((y + 4 - dy) % 4)
        for dz in range(4):
            if dz + dy > 0:
                pl.when(jnp.logical_not(absent[dz]))(r_send(4 * dz + dy).wait_recv)
        projected = rbuf[dy].astype(F32)
        for dz in (1, 2, 3):
            part = rbuf[4 * dz + dy].astype(F32)
            projected = projected + jnp.where(absent[dz], 0.0, part)
        mixed = resbuf[:, at].astype(F32) + gsel[:, at] * projected
        out_ref[:, at] = mixed.astype(BF16)

    finish()

    def r_left(step, carry):
        held = jnp.logical_and(paired((y + step) % 4), across((zl + step // 4) % 4))

        @pl.when(jnp.logical_not(jnp.logical_and(held, outer)))
        def _():
            r_send(step).wait_send()

        return carry

    lax.fori_loop(1, 16, r_left, 0)
    for n in range(len(PAIRED)):
        pl.when(outer)(pair_send(n).wait_send)


def on_device(
    residual_in,
    query_rows,
    key_rows,
    value_rows,
    out_weight,
    gate_table,
    stretch_order,
    noise_levels,
):
    rows, width_in = query_rows.shape
    width = residual_in.shape[1]
    slab = width // 4
    any_spec = pl.BlockSpec(memory_space=pltpu.HBM)
    smem_spec = pl.BlockSpec(memory_space=pltpu.SMEM)
    dma = pltpu.SemaphoreType.DMA
    return pl.pallas_call(
        kernel,
        out_shape=pltpu.VMEM(residual_in.shape, BF16),
        in_specs=[any_spec] * 6 + [smem_spec] * 2,
        out_specs=pl.BlockSpec(memory_space=pltpu.VMEM),
        scratch_shapes=[
            pltpu.VMEM((4, 2, 4, 4, rows // 16, DH), BF16),
            pltpu.VMEM((4, 2, rows, DH), BF16),
            pltpu.VMEM((4, 2, rows, DH), BF16),
            pltpu.VMEM((4, 2, 4, 4, rows // 16, DH), F32),
            pltpu.VMEM((4, 2, 4, 4, rows // 16, DH), F32),
            pltpu.VMEM((4, 2, 4, 4, rows // 16, DH), F32),
            pltpu.VMEM((4, 2, rows, DH), BF16),
            pltpu.VMEM((len(BLOCKS), 4, 8, DH), F32),
            pltpu.VMEM((3, 2, rows, DH), BF16),
            pltpu.VMEM((len(BLOCKS), 3, 8, DH), F32),
            pltpu.VMEM((rows, DH), BF16),
            pltpu.VMEM((rows, 8 * DH), BF16),
            pltpu.VMEM((4 * rows, slab), BF16),
            pltpu.VMEM((rows, slab), BF16),
            pltpu.VMEM((16, 16, slab), BF16),
            pltpu.VMEM((len(PAIRED), 32, slab), BF16),
            pltpu.VMEM(gate_table.shape, BF16),
            pltpu.VMEM((16, width), F32),
            pltpu.VMEM(residual_in.shape, BF16),
            dma((6,)),
            dma((2, 8)),
            dma((2, 4)),
            dma((2, 3)),
            dma((2, 6)),
            dma((2, 3 * len(BLOCKS))),
            dma((2, 3 * len(BLOCKS))),
            dma((2, len(BLOCKS))),
            dma((2, 6 * len(BLOCKS))),
            dma((2, 3)),
            dma((2, 3)),
            dma((2, 16)),
            dma((2, len(PAIRED))),
        ],
        compiler_params=pltpu.CompilerParams(
            collective_id=0, has_side_effects=True, vmem_limit_bytes=62 * 1024 * 1024
        ),
        name="sublayer",
    )(
        residual_in,
        query_rows.reshape(4, 4, rows // 16, width_in),
        key_rows,
        value_rows,
        out_weight,
        gate_table,
        stretch_order,
        noise_levels,
    )


def solution(mesh):
    placed = (
        P(("ctx", "tp"), None),
        P("ctx", "tp"),
        P("ctx", "tp"),
        P("ctx", "tp"),
        P("tp", None),
        P(),
        P(),
        P(),
    )
    return jax.shard_map(
        on_device, mesh=mesh, in_specs=placed, out_specs=P(("ctx", "tp"), None), check_vma=False
    )
```

```python
import functools
import math

import jax
import jax.numpy as jnp
from jax import lax
from jax.experimental import pallas as pl
from jax.experimental.pallas import tpu as pltpu
from jax.sharding import PartitionSpec as P

MESH = pl.DeviceIdType.MESH
DH = 128
NEG = -1e30
BLOCKS = ((0, 1), (1, 3), (3, 4))
PAIRED = (0,)
SCALE = math.log2(math.e) / math.sqrt(DH)
F32 = jnp.float32
BF16 = jnp.bfloat16


def remote(src, dst, sems, device):
    return pltpu.make_async_remote_copy(
        src_ref=src,
        dst_ref=dst,
        send_sem=sems[0],
        recv_sem=sems[1],
        device_id=device,
        device_id_type=MESH,
    )


def kernel(
    res_in,
    q_in,
    k_in,
    v_in,
    w_in,
    gate_in,
    order_ref,
    noise_ref,
    out_ref,
    qbuf,
    kbuf,
    vbuf,
    acc,
    lsum,
    peak,
    osend,
    lsend,
    oret,
    lret,
    zsend,
    abuf,
    wbuf,
    pbuf,
    rbuf,
    sbuf,
    gbuf,
    gsel,
    resbuf,
    local_sem,
    sib_sem,
    par_sem,
    crs_sem,
    qx_sem,
    ox_sem,
    lx_sem,
    z_sem,
    a_sem,
    w_sem,
    wf_sem,
    r_sem,
    s_sem,
):
    ctx = lax.axis_index("ctx")
    tp = lax.axis_index("tp")
    x = ctx // 8
    zh = (ctx // 2) % 4
    core = ctx % 2
    zl = tp // 4
    y = tp % 4
    odd = zl % 2
    ring = (zh + odd) % 4
    head = ring // 2
    mine = pl.ds(pl.multiple_of(head * DH, DH), DH)
    other = pl.ds(pl.multiple_of((1 - head) * DH, DH), DH)

    def at_ring(place):
        return (x * 8 + ((place + 4 - odd) % 4) * 2 + core, tp)

    sib = (ctx + 1 - 2 * core, tp)
    par = at_ring(ring + 1 - 2 * (ring % 2))
    crs = at_ring(3 - ring)
    rows = k_in.shape[0]
    half = rows // 2
    slab = wbuf.shape[1]

    def xpeer(dx):
        return (((x + dx) % 4) * 8 + zh * 2 + core, tp)

    def ypeer(dy):
        return (ctx, zl * 4 + (y + dy) % 4)

    def tpeer(dz, dy):
        return (ctx, ((zl + dz) % 4) * 4 + (y + dy) % 4)

    def columns(index):
        return pl.ds(pl.multiple_of(index * slab, slab), slab)

    started = []

    def send(copy):
        copy.start()
        started.append(copy)

    def got(copy):
        copy.wait_recv()

    def here(index):
        locals_[index].wait()


    def finish():
        for copy in started:
            copy.wait_send()

    locals_ = [
        pltpu.make_async_copy(q_in.at[:, :, :, mine], qbuf.at[0, 0], local_sem.at[0]),
        pltpu.make_async_copy(k_in.at[:, mine], kbuf.at[0, 0], local_sem.at[1]),
        pltpu.make_async_copy(v_in.at[:, mine], vbuf.at[0, 0], local_sem.at[2]),
        pltpu.make_async_copy(w_in.at[:, columns(y)], wbuf.at[pl.ds(0, rows)], local_sem.at[3]),
        pltpu.make_async_copy(gate_in, gbuf, local_sem.at[4]),
        pltpu.make_async_copy(res_in, resbuf, local_sem.at[5]),
    ]
    for copy in locals_:
        copy.start()

    barrier = pltpu.get_barrier_semaphore()
    partners = [sib, par, crs] + [xpeer(dx) for dx in (1, 2, 3)]
    for partner in partners:
        pl.semaphore_signal(barrier, inc=1, device_id=partner, device_id_type=MESH)

    def greet(step, carry):
        pl.semaphore_signal(
            barrier, inc=1, device_id=tpeer(step // 4, step % 4), device_id_type=MESH
        )
        return carry

    lax.fori_loop(1, 16, greet, 0)
    pl.semaphore_wait(barrier, len(partners) + 15)

    q_cross = remote(q_in.at[:, :, :, other], qbuf.at[0, 1], (crs_sem.at[0, 0], crs_sem.at[1, 0]), crs)
    k_cross = remote(k_in.at[:, other], kbuf.at[2, 0], (crs_sem.at[0, 1], crs_sem.at[1, 1]), crs)
    v_cross = remote(v_in.at[:, other], vbuf.at[2, 0], (crs_sem.at[0, 2], crs_sem.at[1, 2]), crs)
    k_pair = remote(k_in.at[:, mine], kbuf.at[1, 0], (par_sem.at[0, 0], par_sem.at[1, 0]), par)
    v_pair = remote(v_in.at[:, mine], vbuf.at[1, 0], (par_sem.at[0, 1], par_sem.at[1, 1]), par)
    k_far = remote(kbuf.at[2, 0], kbuf.at[3, 0], (par_sem.at[0, 2], par_sem.at[1, 2]), par)
    v_far = remote(vbuf.at[2, 0], vbuf.at[3, 0], (par_sem.at[0, 3], par_sem.at[1, 3]), par)

    def share(buf, role, number):
        src = buf.at[role, 0]
        if role == 0:
            src = (k_in if number == 0 else v_in).at[:, mine]
        index = 2 * role + number
        return remote(src, buf.at[role, 1], (sib_sem.at[0, index], sib_sem.at[1, index]), sib)

    k_share = [share(kbuf, role, 0) for role in range(4)]
    v_share = [share(vbuf, role, 1) for role in range(4)]

    @functools.cache
    def q_across(part, dx):
        index = part * 3 + dx - 1
        src = q_in.at[:, :, :, mine] if part == 0 else qbuf.at[0, 1]
        return remote(
            src, qbuf.at[dx, part], (qx_sem.at[0, index], qx_sem.at[1, index]), xpeer(dx)
        )

    @functools.cache
    def w_send(dy):
        own_half = pl.ds(pl.multiple_of(half * core, half), half)
        there = pl.ds(pl.multiple_of(dy * rows + half * core, half), half)
        return remote(
            w_in.at[own_half, columns((y + dy) % 4)],
            wbuf.at[there],
            (w_sem.at[0, dy - 1], w_sem.at[1, dy - 1]),
            ypeer(dy),
        )

    @functools.cache
    def w_share(dy):
        there = pl.ds(pl.multiple_of(dy * rows + half * core, half), half)
        return remote(wbuf.at[there], wbuf.at[there], (wf_sem.at[0, dy - 1], wf_sem.at[1, dy - 1]), sib)

    send(k_pair)
    send(k_cross)
    send(v_pair)
    send(v_cross)
    send(q_cross)
    send(k_share[0])
    send(v_share[0])
    for dx in (1, 2, 3):
        send(q_across(0, dx))
    for dy in (1, 2, 3):
        send(w_send(dy))

    def attend(role, spot, batch):

        def load(ref):
            return ref[spot].reshape(batch, DH)

        k = kbuf[role].reshape(2 * rows, DH)
        v = vbuf[role].reshape(2 * rows, DH)
        count = 2 * rows // DH
        s = (
            lax.dot_general(load(qbuf), k, (((1,), (1,)), ((), ())), preferred_element_type=F32)
            * SCALE
        )
        m = jnp.broadcast_to(jnp.max(s, axis=1, keepdims=True), (batch, DH))
        if role > 0:
            before = load(peak)
            m = jnp.maximum(before, m)
            fade = jnp.exp2(before - m)
        p = jnp.exp2(s - jnp.concatenate([m] * count, axis=1))
        total = p[:, :DH]
        for part in range(1, count):
            total = total + p[:, part * DH : (part + 1) * DH]
        summed = jnp.dot(p.astype(BF16), v, preferred_element_type=F32)
        if role > 0:
            total = total + load(lsum) * fade
            summed = summed + load(acc) * fade
        return m, total, summed

    def attend_part(role, part):
        spot = (slice(None), part)
        m, total, summed = attend(role, spot, 4 * rows)
        for ref, value in ((peak, m), (lsum, total), (acc, summed)):
            ref[spot] = value.reshape(ref[spot].shape)

    here(0)
    here(1)
    here(2)
    got(k_share[0])
    got(v_share[0])
    for dx in (1, 2, 3):
        got(q_across(0, dx))
    attend_part(0, 0)

    got(k_cross)
    send(k_far)
    send(k_share[2])
    got(k_pair)
    send(k_share[1])
    got(v_cross)
    send(v_far)
    send(v_share[2])
    got(v_pair)
    send(v_share[1])
    here(4)
    place = order_ref[x]
    level = noise_ref[0] * 0
    for slot in range(4):
        level = level + jnp.where(place == slot, noise_ref[slot], 0)
    levels = gbuf.shape[0]
    picker = (lax.broadcasted_iota(jnp.int32, (16, levels), 1) == level).astype(BF16)
    for piece in range(4):
        at = pl.ds(piece * slab, slab)
        gsel[:, at] = jnp.dot(picker, gbuf[:, at], preferred_element_type=F32)

    got(q_cross)
    for dx in (1, 2, 3):
        send(q_across(1, dx))
    got(k_share[1])
    got(v_share[1])
    attend_part(1, 0)
    got(k_share[2])
    got(v_share[2])
    attend_part(2, 0)
    for dx in (1, 2, 3):
        got(q_across(1, dx))
    attend_part(0, 1)
    got(k_far)
    send(k_share[3])
    attend_part(1, 1)
    got(v_far)
    send(v_share[3])
    attend_part(2, 1)
    got(k_share[3])
    got(v_share[3])

    def block_rows(j):
        first, past = BLOCKS[j]
        return pl.ds(first * rows // 4, (past - first) * rows // 4)

    @functools.cache
    def o_back(j, dx):
        index = j * 3 + dx - 1
        return remote(
            osend.at[dx, :, block_rows(j)],
            oret.at[dx - 1, :, block_rows(j)],
            (ox_sem.at[0, index], ox_sem.at[1, index]),
            xpeer(4 - dx),
        )

    @functools.cache
    def l_back(j, dx):
        index = j * 3 + dx - 1
        return remote(
            lsend.at[j, dx],
            lret.at[j, dx - 1],
            (lx_sem.at[0, index], lx_sem.at[1, index]),
            xpeer(4 - dx),
        )

    for j, (y_first, y_past) in enumerate(BLOCKS):
        count = y_past - y_first
        size = count * rows // 4
        m, total, summed = attend(
            3, (slice(None), slice(None), slice(None), slice(y_first, y_past)), 8 * size
        )
        total = jnp.sum(total, axis=1, keepdims=True)
        result = (summed * (1.0 / total)).astype(BF16).reshape(4, 2, 4, count, rows // 16, DH)
        lse = (m + jnp.log2(total)).reshape(8, size, DH)
        for dx in range(4):
            for part in (0, 1):
                for step in range(count):
                    there = pl.ds((y_first + step) * rows // 4, rows // 4)
                    osend[dx, part, there] = result[dx, part, :, step].reshape(rows // 4, DH)
                ordered = (
                    lse[2 * dx + part]
                    .reshape(4, count, rows // 16, DH)
                    .swapaxes(0, 1)
                    .reshape(size, DH)
                )
                lsend[j, dx, part : part + 1, :size] = ordered.T[:1]
        for dx in (1, 2, 3):
            send(l_back(j, dx))
            send(o_back(j, dx))
        if j == 0:
            for dy in (1, 2, 3):
                got(w_send(dy))
                send(w_share(dy))


    seen = [order_ref[(x + dx) % 4] <= place for dx in (1, 2, 3)]

    def merged(j, part):
        at = block_rows(j)
        size = at.size
        states = [(lsend[j, 0, part : part + 1, :size], osend[0, part, at])]
        for dx in (1, 2, 3):
            lse = jnp.where(seen[dx - 1], lret[j, dx - 1, part : part + 1, :size], NEG)
            states.append((lse, oret[dx - 1, part, at]))
        highest = states[0][0]
        for lse, _ in states[1:]:
            highest = jnp.maximum(highest, lse)
        shares = [jnp.exp2(lse - highest) for lse, _ in states]
        total = shares[0] + shares[1] + shares[2] + shares[3]
        result = jnp.zeros((size, DH), F32)
        for weight, (_, value) in zip(shares, states):
            result = result + jnp.broadcast_to(weight / total, (DH, size)).T * value.astype(F32)
        return result.astype(BF16)

    @functools.cache
    def back(j):
        at = block_rows(j)
        return remote(zsend.at[at], abuf.at[at, mine], (z_sem.at[0, j], z_sem.at[1, j]), crs)

    @functools.cache
    def a_send(j, which, dy):
        index = (2 * j + which) * 3 + dy - 1
        lane = head if which == 0 else 1 - head
        at = block_rows(j)
        there = pl.ds(pl.multiple_of(dy * 2 * DH + lane * DH, DH), DH)
        return remote(
            abuf.at[at, mine if which == 0 else other],
            abuf.at[at, there],
            (a_sem.at[0, index], a_sem.at[1, index]),
            ypeer(dy),
        )

    every = range(len(BLOCKS))
    for j in every:
        for dx in (1, 2, 3):
            got(l_back(j, dx))
            got(o_back(j, dx))
        zsend[block_rows(j)] = merged(j, 1)
        send(back(j))
        abuf[block_rows(j), mine] = merged(j, 0)
        for dy in (1, 2, 3):
            send(a_send(j, 0, dy))
    for j in every:
        got(back(j))
        for dy in (1, 2, 3):
            send(a_send(j, 1, dy))

    here(3)
    for dy in (1, 2, 3):
        got(w_share(dy))


    piece_width = 512

    def r_send(step):
        there = tpeer(step // 4, step % 4)
        first = pl.ds(pl.multiple_of((there[1] % 4) * 64 + (there[1] // 4) * 16, 16), 16)
        return remote(
            pbuf.at[first], rbuf.at[step], (r_sem.at[0, step], r_sem.at[1, step]), there
        )

    outer = zl % 3 == 0
    buddy = (ctx, (zl + 1 - 2 * (zl % 2)) * 4 + y)

    def paired(to_y):
        result = to_y == PAIRED[0]
        for value in PAIRED[1:]:
            result = jnp.logical_or(result, to_y == value)
        return result

    def across(other_zl):
        return other_zl // 2 != zl // 2

    def pair_rows(n):
        return pl.ds(pl.multiple_of(PAIRED[n] * 64 + 32 * (1 - zl // 2), 32), 32)

    def pair_send(n):
        return remote(pbuf.at[pair_rows(n)], sbuf.at[n], (s_sem.at[0, n], s_sem.at[1, n]), buddy)

    for j, (y_first, y_past) in enumerate(BLOCKS):
        for dy in (1, 2, 3):
            got(a_send(j, 0, dy))
            got(a_send(j, 1, dy))

        def project(i, carry):
            at = pl.ds(pl.multiple_of(i * piece_width, piece_width), piece_width)
            pbuf[block_rows(j), at] = jnp.dot(
                abuf[block_rows(j)], wbuf[:, at], preferred_element_type=F32
            ).astype(BF16)
            return carry

        lax.fori_loop(0, slab // piece_width, project, 0)

        for n, to_y in enumerate(PAIRED):
            if y_first <= to_y < y_past:
                pl.when(outer)(pair_send(n).start)

        count = y_past - y_first

        def r_start(i, carry):
            turn = i // count
            dz = (turn + 2) * (1 - turn // 2) + (3 - turn) * (turn // 2)
            to_y = y_first + i % count
            step = dz * 4 + (to_y + 4 - y) % 4
            later = jnp.logical_and(paired(to_y), across((zl + dz) % 4))

            @pl.when(jnp.logical_and(step != 0, jnp.logical_not(later)))
            def _():
                r_send(step).start()

            return carry

        lax.fori_loop(0, 4 * count, r_start, 0)

    for n, to_y in enumerate(PAIRED):

        @pl.when(jnp.logical_not(outer))
        def _():
            pair_send(n).wait_recv()
            at = pair_rows(n)
            pbuf[at] = (pbuf[at].astype(F32) + sbuf[n].astype(F32)).astype(BF16)
            for which in (0, 1):
                to_zl = 2 * (1 - zl // 2) + which
                r_send((to_zl + 4 - zl) % 4 * 4 + (to_y + 4 - y) % 4).start()

    own_rows = pl.ds(pl.multiple_of(y * 64 + zl * 16, 16), 16)
    rbuf[0] = pbuf[own_rows]

    here(5)
    absent = []
    for dz in range(4):
        from_zl = (zl + 4 - dz) % 4
        absent.append(
            jnp.logical_and(paired(y), jnp.logical_and(across(from_zl), from_zl % 3 == 0))
        )
    for dy in (3, 2, 1, 0):
        at = columns((y + 4 - dy) % 4)
        for dz in range(4):
            if dz + dy > 0:
                pl.when(jnp.logical_not(absent[dz]))(r_send(4 * dz + dy).wait_recv)
        projected = rbuf[dy].astype(F32)
        for dz in (1, 2, 3):
            part = rbuf[4 * dz + dy].astype(F32)
            projected = projected + jnp.where(absent[dz], 0.0, part)
        mixed = resbuf[:, at].astype(F32) + gsel[:, at] * projected
        out_ref[:, at] = mixed.astype(BF16)

    finish()

    def r_left(step, carry):
        held = jnp.logical_and(paired((y + step) % 4), across((zl + step // 4) % 4))

        @pl.when(jnp.logical_not(jnp.logical_and(held, outer)))
        def _():
            r_send(step).wait_send()

        return carry

    lax.fori_loop(1, 16, r_left, 0)
    for n in range(len(PAIRED)):
        pl.when(outer)(pair_send(n).wait_send)


def on_device(
    residual_in,
    query_rows,
    key_rows,
    value_rows,
    out_weight,
    gate_table,
    stretch_order,
    noise_levels,
):
    rows, width_in = query_rows.shape
    width = residual_in.shape[1]
    slab = width // 4
    any_spec = pl.BlockSpec(memory_space=pltpu.HBM)
    smem_spec = pl.BlockSpec(memory_space=pltpu.SMEM)
    dma = pltpu.SemaphoreType.DMA
    return pl.pallas_call(
        kernel,
        out_shape=pltpu.VMEM(residual_in.shape, BF16),
        in_specs=[any_spec] * 6 + [smem_spec] * 2,
        out_specs=pl.BlockSpec(memory_space=pltpu.VMEM),
        scratch_shapes=[
            pltpu.VMEM((4, 2, 4, 4, rows // 16, DH), BF16),
            pltpu.VMEM((4, 2, rows, DH), BF16),
            pltpu.VMEM((4, 2, rows, DH), BF16),
            pltpu.VMEM((4, 2, 4, 4, rows // 16, DH), F32),
            pltpu.VMEM((4, 2, 4, 4, rows // 16, DH), F32),
            pltpu.VMEM((4, 2, 4, 4, rows // 16, DH), F32),
            pltpu.VMEM((4, 2, rows, DH), BF16),
            pltpu.VMEM((len(BLOCKS), 4, 8, DH), F32),
            pltpu.VMEM((3, 2, rows, DH), BF16),
            pltpu.VMEM((len(BLOCKS), 3, 8, DH), F32),
            pltpu.VMEM((rows, DH), BF16),
            pltpu.VMEM((rows, 8 * DH), BF16),
            pltpu.VMEM((4 * rows, slab), BF16),
            pltpu.VMEM((rows, slab), BF16),
            pltpu.VMEM((16, 16, slab), BF16),
            pltpu.VMEM((len(PAIRED), 32, slab), BF16),
            pltpu.VMEM(gate_table.shape, BF16),
            pltpu.VMEM((16, width), F32),
            pltpu.VMEM(residual_in.shape, BF16),
            dma((6,)),
            dma((2, 8)),
            dma((2, 4)),
            dma((2, 3)),
            dma((2, 6)),
            dma((2, 3 * len(BLOCKS))),
            dma((2, 3 * len(BLOCKS))),
            dma((2, len(BLOCKS))),
            dma((2, 6 * len(BLOCKS))),
            dma((2, 3)),
            dma((2, 3)),
            dma((2, 16)),
            dma((2, len(PAIRED))),
        ],
        compiler_params=pltpu.CompilerParams(
            collective_id=0, has_side_effects=True, vmem_limit_bytes=62 * 1024 * 1024
        ),
        name="sublayer",
    )(
        residual_in,
        query_rows.reshape(4, 4, rows // 16, width_in),
        key_rows,
        value_rows,
        out_weight,
        gate_table,
        stretch_order,
        noise_levels,
    )


def solution(mesh):
    placed = (
        P(("ctx", "tp"), None),
        P("ctx", "tp"),
        P("ctx", "tp"),
        P("ctx", "tp"),
        P("tp", None),
        P(),
        P(),
        P(),
    )
    return jax.shard_map(
        on_device, mesh=mesh, in_specs=placed, out_specs=P(("ctx", "tp"), None), check_vma=False
    )
```
